512 devices in a mesh: dp: 16 (over y_lo, x, core), code: 32 (over y_hi, z).
Axes of the slice: x: 4, y: 4 (y_hi: 2, y_lo: 2; y = y_hi * 2 + y_lo), z: 16, core: 2. Of those that a mesh axis runs over, the one named last changes fastest.
Arguments:
- features: bfloat16 [65536, 768], P('dp'), may hold values from -8 to 8
- centroids: bfloat16 [131072, 768], P(('code', 'dp')), may hold values from -4.7 to 4.7
- block_lists: int32 [128, 32], P('dp'), may hold values from 0 to 511, as said below
Outputs:
- new_centroids: bfloat16 [131072, 768], P(('code', 'dp'))
- column_mass: float32 [131072], P(('code', 'dp'))
The draws below stay inside these ranges and needn't reach their ends.
Inputs may be any that keep to these rules, and one draw needn't show every extreme that they name: Let i = b // 8 for feature block b. Slot s of block_lists[b] names a block s * 16 + (i + e) mod 16 with e one of -1, 0, 1; in every slot, the 8 feature blocks with the same i together name all three such blocks.
All inputs are finite; a program needn't handle non-finite values.
Results may differ from the reference program's by a relative error of at most 0.0055.
The reference program's roundings to bfloat16 on the way count: a program that leaves them out, or rounds other values in their place, can miss the bound.
Values may be sent and summed in bfloat16 or wider, within the bound.
A program may use at most 64 MiB of HBM per device.

```python
import math
import jax
import jax.numpy as jnp
from jax import lax

D = 768
CB = 256
FB = 512
ROUNDS = 3
FBD = 8
LIST = 32
N = 65536
K = 131072
NB = 512
NFB = 128
N_DP = 16


def make_lists(key):
    key_a, key_b = jax.random.split(jax.random.fold_in(key, 101), 2)
    spots = jnp.arange(FBD, dtype=jnp.int32)[None, None, :]
    extra = jax.random.randint(key_a, (N_DP, LIST, FBD), -1, 2)
    offsets = jnp.where(spots < 3, spots - 1, extra)
    scores = jax.random.randint(key_b, (N_DP, LIST, FBD), 0, 1 << 20) * FBD + spots
    order = jnp.argsort(scores, axis=2)
    offsets = jnp.take_along_axis(offsets, order, axis=2)
    dp_rows = jnp.arange(N_DP, dtype=jnp.int32)[:, None, None]
    groups = jnp.arange(LIST, dtype=jnp.int32)[None, :, None]
    ids = groups * N_DP + (dp_rows + offsets) % N_DP
    return jnp.transpose(ids, (0, 2, 1)).reshape(NFB, LIST).astype(jnp.int32)


def centroid_base(key):
    base = jnp.clip(jax.random.normal(jax.random.fold_in(key, 202), (K, D), jnp.float32), -4.0, 4.0)
    table = base.reshape(NB, CB, D)
    level = min(4.4, math.sqrt(620.0 / D))
    first = jnp.where(table[:, 0] >= 0.0, level, -level)
    second = jnp.where(table[:, 2] >= 0.0, level, -level)
    table = table.at[:, 0].set(first)
    table = table.at[:, 2].set(second)
    return table.reshape(K, D)


def aligned_rows(plain, lists, base):
    picked = base.reshape(NB, CB, D)[lists[:, 0]]
    plain = plain.at[:, 0].set(1.8 * picked[:, 0])
    plain = plain.at[:, 1].set(1.7 * picked[:, 2])
    plain = plain.at[:, 2].set(1.6 * picked[:, 0])
    return plain


def draw_block_lists(key, part):
    return make_lists(key)


def draw_centroids(key, part):
    base = centroid_base(key)
    return base.astype(jnp.bfloat16)


def draw_features(key, part):
    lists = make_lists(key)
    base = centroid_base(key)
    key = jax.random.fold_in(key, 5)
    plain = jnp.clip(jax.random.normal(key, (NFB, FB, D), jnp.float32), -4.0, 4.0)
    plain = aligned_rows(plain, lists, base)
    return plain.reshape(N, D).astype(jnp.bfloat16)


def setup_inputs(seed: int = 0) -> dict:
    key_of = jax.random.split(jax.random.key(seed), 4)
    features = draw_features(jax.random.fold_in(key_of[3], 71), 0)
    centroids = draw_centroids(jax.random.fold_in(key_of[3], 71), 0)
    block_lists = draw_block_lists(jax.random.fold_in(key_of[3], 71), 0)
    return {"features": features, "centroids": centroids, "block_lists": block_lists}


SOFTMAX_TEMP = 12.0


def reference(features, centroids, block_lists):
    block_table = centroids.reshape(NB, CB, D)
    norm_table = jnp.sum(jnp.square(centroids.astype(jnp.float32)), axis=1).reshape(NB, CB)
    feat_blocks = features.reshape(NFB, FB, D)
    flat_ids = block_lists.reshape(NFB * LIST)
    log_target = jnp.log(jnp.float32(N) / jnp.float32(K))

    def score_block(pair):
        feat_rows, listed_row = pair
        picked = block_table[listed_row].reshape(LIST * CB, D)
        return lax.dot_general(feat_rows, picked, (((1,), (1,)), ((), ())), preferred_element_type=jnp.float32).astype(jnp.bfloat16)

    inner_product = lax.map(score_block, (feat_blocks, block_lists))

    def block_score_logits(inner_feature_rows, listed_row):
        listed_norm = norm_table[listed_row].reshape(1, LIST * CB)
        return (2.0 * inner_feature_rows.astype(jnp.float32) - listed_norm) / SOFTMAX_TEMP

    def row_potential(col_pot):
        def one_block(item):
            inner_feature_rows, listed_row = item
            shifted = block_score_logits(inner_feature_rows, listed_row) + col_pot[listed_row].reshape(1, LIST * CB)
            row_peak = jnp.max(shifted, axis=1)
            row_total = jnp.sum(jnp.exp(shifted - row_peak[:, None]), axis=1)
            return -(row_peak + jnp.log(row_total))
        return lax.map(one_block, (inner_product, block_lists))

    def col_potential(row_pot):
        def block_peak(item):
            inner_feature_rows, listed_row, row_values = item
            shifted = (block_score_logits(inner_feature_rows, listed_row) + row_values[:, None]).reshape(FB, LIST, CB)
            return jnp.max(shifted, axis=0)
        peaks = lax.map(block_peak, (inner_product, block_lists, row_pot)).reshape(NFB * LIST, CB)
        col_peak = jax.ops.segment_max(peaks, flat_ids, num_segments=NB)

        def block_total(item):
            inner_feature_rows, listed_row, row_values = item
            shifted = (block_score_logits(inner_feature_rows, listed_row) + row_values[:, None]).reshape(FB, LIST, CB)
            return jnp.sum(jnp.exp(shifted - col_peak[listed_row][None, :, :]), axis=0)
        totals = lax.map(block_total, (inner_product, block_lists, row_pot)).reshape(NFB * LIST, CB)
        col_total = jax.ops.segment_sum(totals, flat_ids, num_segments=NB)
        return log_target - (col_peak + jnp.log(col_total))

    col_pot = jnp.zeros((NB, CB), jnp.float32)
    for sweep_index in range(ROUNDS):
        row_pot = row_potential(col_pot)
        col_pot = col_potential(row_pot)
    row_pot = row_potential(col_pot)

    def add_block(part_carry, item):
        numer_part, mass_part = part_carry
        inner_feature_rows, listed_row, row_values, feat_rows = item
        weights = jnp.exp(block_score_logits(inner_feature_rows, listed_row) + row_values[:, None] + col_pot[listed_row].reshape(1, LIST * CB))
        weight_low = weights.astype(jnp.bfloat16)
        numer_rows = jnp.dot(weight_low.T, feat_rows, preferred_element_type=jnp.float32).reshape(LIST, CB, D)
        numer_part = numer_part.at[listed_row].add(numer_rows)
        mass_part = mass_part.at[listed_row].add(jnp.sum(weights, axis=0).reshape(LIST, CB))
        return (numer_part, mass_part), None

    def add_index(carry, item):
        numer_acc, mass_acc = carry
        start_part = (jnp.zeros((NB, CB, D), jnp.float32), jnp.zeros((NB, CB), jnp.float32))
        (numer_part, mass_part), unused = lax.scan(add_block, start_part, item)
        numer_acc = numer_acc + lax.optimization_barrier(numer_part.astype(jnp.bfloat16)).astype(jnp.float32)
        mass_acc = mass_acc + lax.optimization_barrier(mass_part.astype(jnp.bfloat16)).astype(jnp.float32)
        return (numer_acc, mass_acc), None

    index_items = (inner_product.reshape(N_DP, FBD, FB, LIST * CB), block_lists.reshape(N_DP, FBD, LIST), row_pot.reshape(N_DP, FBD, FB), feat_blocks.reshape(N_DP, FBD, FB, D))
    start_carry = (jnp.zeros((NB, CB, D), jnp.float32), jnp.zeros((NB, CB), jnp.float32))
    (numer_total, mass_total), unused = lax.scan(add_index, start_carry, index_items)
    new_centroids = (numer_total / mass_total[..., None]).astype(jnp.bfloat16).reshape(K, D)
    return new_centroids, mass_total.reshape(K)
```

```python
import functools
import math

import jax
import jax.numpy as jnp
from jax import lax
from jax.experimental import pallas as pl
from jax.experimental.pallas import tpu as pltpu
from jax.sharding import PartitionSpec as P

ROUNDS = 3
SOFTMAX_TEMP = 12.0
LOG2E = math.log2(math.e)
LOWEST = -3.0e38
LANES = 128
SUB = 8
PIECES = 3
MESH = pl.DeviceIdType.MESH


def kernel(
    n_dp,
    n_code,
    lists_ref,
    feat_hbm,
    cent_hbm,
    out_ref,
    mass_ref,
    feat,
    win,
    cells,
    row_b,
    col_b,
    peak,
    total,
    weight,
    lse_src,
    lse_in,
    row_src,
    row_in,
    col_src,
    col_l2,
    col_l1,
    col_r1,
    col_r2,
    mass_src,
    mass_in,
    num_src,
    num_in,
    num_own,
    feat_sem,
    own_sem,
    halo_send,
    halo_recv,
    lse_send,
    lse_recv,
    row_send,
    row_recv,
    col_send,
    col_recv,
    mass_send,
    mass_recv,
    num_send,
    num_recv,
):
    dp = lax.axis_index("dp")
    code = lax.axis_index("code")
    blocks = lists_ref.shape[0]
    rows = feat.shape[0]
    block_rows = rows // blocks
    block_tiles = block_rows // LANES
    tiles = rows // LANES
    size, width = win.shape[1], win.shape[2]
    halves = size // LANES
    piece = width // PIECES
    odd = lax.rem(dp, 2)

    def dp_at(step):
        return lax.rem(dp + (n_dp + step), n_dp)

    def place(b):
        return jnp.minimum(lax.rem(lists_ref[b, code] + (n_dp + 1) - dp, n_dp), 2)

    def feat_copy(b):
        span = pl.ds(b * block_rows, block_rows)
        return pltpu.make_async_copy(feat_hbm.at[span], feat.at[span], feat_sem.at[b])

    def remote(src, dst, send, recv, to_dp, to_code):
        return pltpu.make_async_remote_copy(
            src_ref=src,
            dst_ref=dst,
            send_sem=send,
            recv_sem=recv,
            device_id=(to_dp, to_code),
            device_id_type=MESH,
        )

    own_copy = pltpu.make_async_copy(cent_hbm, win.at[1], own_sem)
    own_copy.start()
    for b in range(blocks):
        feat_copy(b).start()

    barrier = pltpu.get_barrier_semaphore()
    for step in (-2, -1, 1, 2):
        pl.semaphore_signal(
            barrier, inc=1, device_id=(dp_at(step), code), device_id_type=MESH
        )

    def greet(j, carry):
        to = lax.rem(code + 1 + j, n_code)
        pl.semaphore_signal(barrier, inc=1, device_id=(dp, to), device_id_type=MESH)
        return carry

    lax.fori_loop(0, n_code - 1, greet, 0)
    pl.semaphore_wait(barrier, n_code - 1 + 4)

    def side(s):
        return 2 * lax.rem(odd + s, 2)

    def halo(s):
        w = side(s)
        return remote(
            cent_hbm,
            win.at[2 - w],
            halo_send.at[s],
            halo_recv.at[1 - w // 2],
            dp_at(w - 1),
            code,
        )

    halo(0).start()
    halo(1).start()
    own_copy.wait()
    for s in range(2):
        halo(s).wait_send()
    for s in range(2):
        remote(cent_hbm, win.at[2 * s], halo_send.at[s], halo_recv.at[s], dp, code).wait_recv()

    eye = lax.broadcasted_iota(jnp.int32, (LANES, LANES), 0) == lax.broadcasted_iota(
        jnp.int32, (LANES, LANES), 1
    )

    def to_lanes(column):
        square = column.reshape(3 * halves, LANES, LANES)
        flat = jnp.sum(jnp.where(eye[None], square, 0.0), axis=1)
        return flat.reshape(3, halves, LANES)

    def to_column(row):
        square = jnp.where(eye, jnp.broadcast_to(row, (LANES, LANES)), 0.0)
        return jnp.broadcast_to(jnp.sum(square, axis=1, keepdims=True), (LANES, LANES))

    def norms(w, carry):
        wide = win[w].astype(jnp.float32)
        norm = jnp.sum(wide * wide, axis=1, keepdims=True)
        col_b[w] = jnp.broadcast_to(norm * (-LOG2E / SOFTMAX_TEMP), (size, LANES))
        return carry

    lax.fori_loop(0, 3, norms, 0)

    def score(b, carry):
        feat_copy(b).wait()
        inner = lax.dot_general(
            win[place(b)],
            feat[pl.ds(pl.multiple_of(b * block_rows, block_rows), block_rows), :],
            (((1,), (1,)), ((), ())),
            preferred_element_type=jnp.float32,
        )
        scaled = inner.astype(jnp.bfloat16).astype(jnp.float32) * (2.0 * LOG2E / SOFTMAX_TEMP)
        for t in range(block_tiles):
            cells[b * block_tiles + t] = scaled[:, t * LANES : (t + 1) * LANES]
        return carry

    lax.fori_loop(0, blocks, score, 0)

    group = 4

    def row_update(r):
        def some_tiles(step, carry):
            ids = [lax.rem(code + 1 + step * group + u, n_code) for u in range(group)]
            for d in ids:
                x = cells[d] + col_b[place(d // block_tiles)]
                x = x.reshape(size // SUB, SUB, LANES)
                m8 = jnp.max(x, axis=0)
                s8 = jnp.sum(jnp.exp2(x - m8[None]), axis=0)
                m = jnp.max(m8, axis=0, keepdims=True)
                s = jnp.sum(s8 * jnp.exp2(m8 - m), axis=0, keepdims=True)
                lse_src[r, d] = m + jnp.log2(s)
            for u, d in enumerate(ids):

                @pl.when(step * group + u < n_code - 1)
                def _():
                    remote(
                        lse_src.at[r, d], lse_in.at[r, code], lse_send.at[r], lse_recv.at[r], dp, d
                    ).start()

            return carry

        lax.fori_loop(0, tiles // group, some_tiles, 0)
        lse_in[r, code] = lse_src[r, code]
        some = pl.ds(0, n_code - 1)
        all_in = remote(
            lse_src.at[r, some], lse_in.at[r, some], lse_send.at[r], lse_recv.at[r], dp, code
        )
        all_in.wait_recv()
        parts = lse_in[r]
        m = jnp.max(parts, axis=0)
        s = jnp.sum(jnp.exp2(parts - m[None]), axis=0)
        value = -(m + jnp.log2(s))
        row_src[r] = value
        row_in[r, code] = value

        def tell(j, carry):
            to = lax.rem(code + 1 + j, n_code)
            remote(
                row_src.at[r], row_in.at[r, code], row_send.at[r], row_recv.at[r], dp, to
            ).start()
            return carry

        lax.fori_loop(0, n_code - 1, tell, 0)
        all_in.wait_send()
        all_rows = remote(
            lse_src.at[r, some], row_in.at[r, some], row_send.at[r], row_recv.at[r], dp, code
        )
        all_rows.wait_recv()
        row_b[...] = jnp.broadcast_to(row_in[r], row_b.shape)
        all_rows.wait_send()

    def col_update(r, target):
        def some_cols(j, carry):
            span = pl.ds(pl.multiple_of(j * SUB, SUB), SUB)
            x = cells[:, span, :] + row_b[...]
            x = x.reshape(blocks, block_tiles, SUB, LANES)
            places = [jnp.full((SUB, LANES), place(b), jnp.int32) for b in range(blocks)]
            tops = [jnp.max(x[b], axis=0) for b in range(blocks)]
            peaks = []
            for w in range(3):
                held = [jnp.where(places[b] == w, tops[b], LOWEST) for b in range(blocks)]
                peaks.append(functools.reduce(jnp.maximum, held))
            sums = []
            for b in range(blocks):
                top = jnp.where(
                    places[b] == 0, peaks[0], jnp.where(places[b] == 1, peaks[1], peaks[2])
                )
                sums.append(jnp.sum(jnp.exp2(x[b] - top[None]), axis=0))
            for w in range(3):
                held = [jnp.where(places[b] == w, sums[b], 0.0) for b in range(blocks)]
                peak[w, span, :] = peaks[w]
                total[w, span, :] = functools.reduce(jnp.add, held)
            return carry

        lax.fori_loop(0, size // SUB, some_cols, 0)
        m = jnp.max(peak[...], axis=2, keepdims=True)
        s = jnp.sum(total[...] * jnp.exp2(peak[...] - m), axis=2, keepdims=True)
        mine = to_lanes(jnp.broadcast_to(m, peak.shape)) + jnp.log2(
            to_lanes(jnp.broadcast_to(s, total.shape))
        )
        col_src[r] = mine
        copies = [
            remote(
                col_src.at[r, pl.ds(start, count)],
                there.at[r],
                col_send.at[r, slot],
                col_recv.at[r, slot],
                dp_at(step),
                code,
            )
            for slot, (step, start, count, there) in enumerate(
                ((-2, 0, 1, col_r2), (2, 2, 1, col_l2), (-1, 0, 2, col_r1), (1, 1, 2, col_l1))
            )
        ]
        for copy in copies:
            copy.start()
        for copy in copies:
            copy.wait_recv()
        l1, r1 = col_l1[r], col_r1[r]
        sets = (
            (col_l2[r, 0], l1[0], mine[0]),
            (l1[1], mine[1], r1[0]),
            (mine[2], r1[1], col_r2[r, 0]),
        )
        for w, terms in enumerate(sets):
            m = functools.reduce(jnp.maximum, terms)
            s = functools.reduce(jnp.add, [jnp.exp2(term - m) for term in terms])
            value = target - (m + jnp.log2(s))
            for h in range(halves):
                col_b[w, h * LANES : (h + 1) * LANES, :] = to_column(value[h : h + 1])
        for copy in copies:
            copy.wait_send()

    target = math.log2((rows * n_dp) / (size * n_dp * n_code))

    def sweep(r, carry):
        row_update(r)
        col_update(r, target)
        return carry

    lax.fori_loop(0, ROUNDS, sweep, 0)
    row_update(ROUNDS)

    pack = 2 * SUB

    def weigh(j, carry):
        span = pl.ds(pl.multiple_of(j * pack, pack), pack)
        sums = [jnp.zeros((2, SUB, LANES), jnp.float32) for w in range(3)]
        for b in range(blocks):
            at = place(b)
            at_b = jnp.full((2, SUB, LANES), at, jnp.int32)
            g = col_b[at, span, :].reshape(2, SUB, LANES)
            here = jnp.zeros((2, SUB, LANES), jnp.float32)
            for t in range(block_tiles):
                d = b * block_tiles + t
                x = cells[d, span, :].reshape(2, SUB, LANES) + row_b[d][None] + g
                value = jnp.exp2(x)
                here = here + value
                for w in range(3):
                    kept = jnp.where(at_b == w, value, 0.0).reshape(pack, LANES)
                    weight[w, span, d * LANES : (d + 1) * LANES] = kept.astype(jnp.bfloat16)
            for w in range(3):
                sums[w] = sums[w] + jnp.where(at_b == w, here, 0.0)
        for w in range(3):
            total[w, span, :] = sums[w].reshape(pack, LANES)
        return carry

    lax.fori_loop(0, size // pack, weigh, 0)

    mass = jnp.sum(total[...], axis=2, keepdims=True)
    mass = to_lanes(jnp.broadcast_to(mass, total.shape))
    mass_src[...] = mass.astype(jnp.bfloat16).astype(jnp.float32)
    mass_copies = [
        remote(
            mass_src.at[pl.ds(2 * s, 1)],
            mass_in.at[1 - s],
            mass_send.at[s],
            mass_recv.at[1 - s],
            dp_at(2 * s - 1),
            code,
        )
        for s in range(2)
    ]
    for copy in mass_copies:
        copy.start()

    def columns(n):
        return pl.ds(pl.multiple_of(n * piece, piece), piece)

    def numerator(w, n):
        return jnp.dot(weight[w], feat[:, columns(n)], preferred_element_type=jnp.float32)

    def num_copy(s, n):
        w = side(s)
        return remote(
            num_src.at[s, n],
            num_in.at[1 - w // 2, n],
            num_send.at[s, n],
            num_recv.at[1 - w // 2, n],
            dp_at(w - 1),
            code,
        )

    def give(q, carry):
        s, n = q // PIECES, lax.rem(q, PIECES)
        num_src[s, n] = numerator(side(s), n).astype(jnp.bfloat16)
        num_copy(s, n).start()
        return carry

    lax.fori_loop(0, 2 * PIECES, give, 0)

    def keep(n, carry):
        num_own[n] = numerator(1, n).astype(jnp.bfloat16).astype(jnp.float32)
        return carry

    lax.fori_loop(0, PIECES, keep, 0)

    for s in range(2):
        remote(
            mass_src.at[pl.ds(0, 1)], mass_in.at[s], mass_send.at[s], mass_recv.at[s], dp, code
        ).wait_recv()
    for copy in mass_copies:
        copy.wait_send()
    mass_all = mass_in[0, 0] + mass_src[1] + mass_in[1, 0]
    mass_ref[...] = mass_all
    for h in range(halves):
        peak[0, h * LANES : (h + 1) * LANES, :] = to_column(mass_all[h : h + 1])

    def finish(n, carry):
        for s in range(2):
            remote(
                num_src.at[s, n], num_in.at[s, n], num_send.at[s, n], num_recv.at[s, n], dp, code
            ).wait()
        whole = (
            num_in[0, n].astype(jnp.float32) + num_own[n] + num_in[1, n].astype(jnp.float32)
        )
        divisor = jnp.concatenate([peak[0]] * (piece // LANES), axis=1)
        out_ref[:, columns(n)] = (whole / divisor).astype(jnp.bfloat16)
        return carry

    lax.fori_loop(0, PIECES, finish, 0)


def solution(mesh):
    n_dp, n_code = mesh.shape["dp"], mesh.shape["code"]

    def local(features, centroids, block_lists):
        rows, width = features.shape
        size = centroids.shape[0]
        tiles = rows // LANES
        halves = size // LANES
        piece = width // PIECES
        updates = ROUNDS + 1
        f32, bf16 = jnp.float32, jnp.bfloat16
        dma = pltpu.SemaphoreType.DMA
        new_centroids, mass = pl.pallas_call(
            functools.partial(kernel, n_dp, n_code),
            out_shape=(
                jax.ShapeDtypeStruct((size, width), bf16),
                jax.ShapeDtypeStruct((halves, LANES), f32),
            ),
            in_specs=[
                pl.BlockSpec(memory_space=pltpu.SMEM),
                pl.BlockSpec(memory_space=pl.ANY),
                pl.BlockSpec(memory_space=pl.ANY),
            ],
            out_specs=(
                pl.BlockSpec(memory_space=pltpu.VMEM),
                pl.BlockSpec(memory_space=pltpu.VMEM),
            ),
            scratch_shapes=[
                pltpu.VMEM((rows, width), bf16),
                pltpu.VMEM((3, size, width), bf16),
                pltpu.VMEM((tiles, size, LANES), f32),
                pltpu.VMEM((tiles, SUB, LANES), f32),
                pltpu.VMEM((3, size, LANES), f32),
                pltpu.VMEM((3, size, LANES), f32),
                pltpu.VMEM((3, size, LANES), f32),
                pltpu.VMEM((3, size, rows), bf16),
                pltpu.VMEM((updates, tiles, 1, LANES), f32),
                pltpu.VMEM((updates, tiles, 1, LANES), f32),
                pltpu.VMEM((updates, 1, LANES), f32),
                pltpu.VMEM((updates, tiles, 1, LANES), f32),
                pltpu.VMEM((ROUNDS, 3, halves, LANES), f32),
                pltpu.VMEM((ROUNDS, 1, halves, LANES), f32),
                pltpu.VMEM((ROUNDS, 2, halves, LANES), f32),
                pltpu.VMEM((ROUNDS, 2, halves, LANES), f32),
                pltpu.VMEM((ROUNDS, 1, halves, LANES), f32),
                pltpu.VMEM((3, halves, LANES), f32),
                pltpu.VMEM((2, 1, halves, LANES), f32),
                pltpu.VMEM((2, PIECES, size, piece), bf16),
                pltpu.VMEM((2, PIECES, size, piece), bf16),
                pltpu.VMEM((PIECES, size, piece), f32),
                dma((block_lists.shape[0],)),
                dma,
                dma((2,)),
                dma((2,)),
                dma((updates,)),
                dma((updates,)),
                dma((updates,)),
                dma((updates,)),
                dma((ROUNDS, 4)),
                dma((ROUNDS, 4)),
                dma((2,)),
                dma((2,)),
                dma((2, PIECES)),
                dma((2, PIECES)),
            ],
            compiler_params=pltpu.CompilerParams(
                collective_id=0, has_side_effects=True, vmem_limit_bytes=56 * 1024 * 1024
            ),
            cost_estimate=pl.CostEstimate(
                flops=8 * rows * size * width,
                bytes_accessed=2 * (rows + 2 * size) * width,
                transcendentals=8 * rows * size,
            ),
            name="balanced_kmeans",
        )(block_lists, features, centroids)
        return new_centroids, mass.reshape(size)

    return jax.shard_map(
        local,
        mesh=mesh,
        in_specs=(P("dp", None), P(("code", "dp"), None), P("dp", None)),
        out_specs=(P(("code", "dp"), None), P(("code", "dp"))),
        check_vma=False,
    )
```

```python
import functools
import math

import jax
import jax.numpy as jnp
from jax import lax
from jax.experimental import pallas as pl
from jax.experimental.pallas import tpu as pltpu
from jax.sharding import PartitionSpec as P

ROUNDS = 3
SOFTMAX_TEMP = 12.0
LOG2E = math.log2(math.e)
LOWEST = -3.0e38
LANES = 128
SUB = 8
PIECES = 3
Z = 16
NEAR = 4
MESH = pl.DeviceIdType.MESH


def kernel(
    n_dp,
    n_code,
    lists_ref,
    feat_hbm,
    cent_hbm,
    whole_ref,
    mass_ref,
    feat,
    win,
    cells,
    row_b,
    col_b,
    peak,
    total,
    weight,
    lse_src,
    lse_in,
    mid_src,
    mid_in,
    row_src,
    row_in,
    col_src,
    col_l2,
    col_l1,
    col_r1,
    col_r2,
    mass_src,
    mass_in,
    num_src,
    num_in,
    num_own,
    feat_sem,
    own_sem,
    halo_send,
    halo_recv,
    lse_send,
    lse_recv,
    mid_send,
    mid_recv,
    row_send,
    row_recv,
    col_send,
    col_recv,
    mass_send,
    mass_recv,
    num_send,
    num_recv,
):
    dp = lax.axis_index("dp")
    code = lax.axis_index("code")
    blocks = lists_ref.shape[0]
    rows = feat.shape[0]
    block_rows = rows // blocks
    block_tiles = block_rows // LANES
    tiles = rows // LANES
    size, width = win.shape[1], win.shape[2]
    halves = size // LANES
    piece = width // PIECES
    odd = lax.rem(dp, 2)

    y_hi, z = code // Z, lax.rem(code, Z)
    quarter, near = z // NEAR, lax.rem(z, NEAR)
    quarters, shares = Z // NEAR, NEAR * (n_code // Z)
    share = y_hi * NEAR + near

    def mate(other):
        return (other // NEAR) * Z + quarter * NEAR + lax.rem(other, NEAR)

    def far_mate(other):
        return y_hi * Z + other * NEAR + near

    def dp_at(step):
        return lax.rem(dp + (n_dp + step), n_dp)

    def place(b):
        return jnp.minimum(lax.rem(lists_ref[b, code] + (n_dp + 1) - dp, n_dp), 2)

    def feat_copy(b):
        span = pl.ds(b * block_rows, block_rows)
        return pltpu.make_async_copy(feat_hbm.at[span], feat.at[span], feat_sem.at[b])

    def remote(src, dst, send, recv, to_dp, to_code):
        return pltpu.make_async_remote_copy(
            src_ref=src,
            dst_ref=dst,
            send_sem=send,
            recv_sem=recv,
            device_id=(to_dp, to_code),
            device_id_type=MESH,
        )

    own_copy = pltpu.make_async_copy(cent_hbm, win.at[1], own_sem)
    own_copy.start()
    for b in range(blocks):
        feat_copy(b).start()

    barrier = pltpu.get_barrier_semaphore()
    for step in (-1, 1, -2, 2):
        pl.semaphore_signal(
            barrier, inc=1, device_id=(dp_at(step), code), device_id_type=MESH
        )
    for step in range(1, shares):
        pl.semaphore_signal(
            barrier, inc=1, device_id=(dp, mate((share + step) % shares)), device_id_type=MESH
        )
    for step in range(1, quarters):
        to = far_mate((quarter + step) % quarters)
        pl.semaphore_signal(barrier, inc=1, device_id=(dp, to), device_id_type=MESH)
    pl.semaphore_wait(barrier, 4 + shares - 1 + quarters - 1)

    def side(s):
        return 2 * lax.rem(odd + s, 2)

    def halo(s):
        w = side(s)
        return remote(
            cent_hbm,
            win.at[2 - w],
            halo_send.at[s],
            halo_recv.at[1 - w // 2],
            dp_at(w - 1),
            code,
        )

    halo(0).start()
    halo(1).start()

    def norms(w):
        wide = win[w].astype(jnp.float32)
        norm = jnp.sum(wide * wide, axis=1, keepdims=True)
        col_b[w] = jnp.broadcast_to(norm * (-LOG2E / SOFTMAX_TEMP), (size, LANES))

    own_copy.wait()
    norms(1)
    for s in range(2):
        halo(s).wait_send()
    for s in range(2):
        remote(cent_hbm, win.at[2 * s], halo_send.at[s], halo_recv.at[s], dp, code).wait_recv()

    eye = lax.broadcasted_iota(jnp.int32, (LANES, LANES), 0) == lax.broadcasted_iota(
        jnp.int32, (LANES, LANES), 1
    )

    def to_lanes(column):
        square = column.reshape(3 * halves, LANES, LANES)
        flat = jnp.sum(jnp.where(eye[None], square, 0.0), axis=1)
        return flat.reshape(3, halves, LANES)

    def to_column(row):
        square = jnp.where(eye, jnp.broadcast_to(row, (LANES, LANES)), 0.0)
        return jnp.broadcast_to(jnp.sum(square, axis=1, keepdims=True), (LANES, LANES))

    def score(b, carry):
        feat_copy(b).wait()
        inner = lax.dot_general(
            win[place(b)],
            feat[pl.ds(pl.multiple_of(b * block_rows, block_rows), block_rows), :],
            (((1,), (1,)), ((), ())),
            preferred_element_type=jnp.float32,
        )
        scaled = inner.astype(jnp.bfloat16).astype(jnp.float32) * (2.0 * LOG2E / SOFTMAX_TEMP)
        for t in range(block_tiles):
            cells[b * block_tiles + t] = scaled[:, t * LANES : (t + 1) * LANES]
        return carry

    lax.fori_loop(0, blocks, score, 0)
    norms(0)
    norms(2)

    def row_block(r, b):
        bias = col_b[place(b)]
        for t in range(block_tiles):
            x = (cells[b * block_tiles + t] + bias).reshape(size // SUB, SUB, LANES)
            m8 = jnp.max(x, axis=0)
            s8 = jnp.sum(jnp.exp2(x - m8[None]), axis=0)
            m = jnp.max(m8, axis=0, keepdims=True)
            s = jnp.sum(s8 * jnp.exp2(m8 - m), axis=0, keepdims=True)
            lse_src[r, b, t : t + 1, :] = m + jnp.log2(s)

    def join(parts):
        m = jnp.max(parts, axis=0)
        return m + jnp.log2(jnp.sum(jnp.exp2(parts - m[None]), axis=0))

    def row_update(r):
        def one_block(step, carry):
            b = lax.rem(share + 1 + step, shares)
            row_block(r, b)
            remote(
                lse_src.at[r, b],
                lse_in.at[r, share],
                lse_send.at[r],
                lse_recv.at[r],
                dp,
                mate(b),
            ).start()
            return carry

        lax.fori_loop(0, shares - 1, one_block, 0)
        row_block(r, share)
        lse_in[r, share] = lse_src[r, share]
        others = pl.ds(0, shares - 1)
        first = remote(
            lse_src.at[r, others], lse_in.at[r, others], lse_send.at[r], lse_recv.at[r], dp, code
        )
        first.wait_recv()
        value = join(lse_in[r])
        mid_src[r] = value
        for step in range(1, quarters):
            remote(
                mid_src.at[r],
                mid_in.at[r, quarter],
                mid_send.at[r],
                mid_recv.at[r],
                dp,
                far_mate((quarter + step) % quarters),
            ).start()
        mid_in[r, quarter] = value
        some = pl.ds(0, quarters - 1)
        second = remote(
            mid_in.at[r, some], mid_in.at[r, some], mid_send.at[r], mid_recv.at[r], dp, code
        )
        second.wait_recv()
        value = -join(mid_in[r])
        row_src[r] = value
        for step in range(1, shares):
            remote(
                row_src.at[r],
                row_in.at[r, share],
                row_send.at[r],
                row_recv.at[r],
                dp,
                mate((share + step) % shares),
            ).start()
        row_in[r, share] = value
        first.wait_send()
        second.wait_send()
        third = remote(
            row_in.at[r, others], row_in.at[r, others], row_send.at[r], row_recv.at[r], dp, code
        )
        third.wait_recv()
        for b in range(blocks):
            for t in range(block_tiles):
                row_b[b * block_tiles + t] = jnp.broadcast_to(
                    row_in[r, b, t : t + 1, :], (SUB, LANES)
                )
        third.wait_send()

    def col_update(r, target):
        def some_cols(j, carry):
            span = pl.ds(pl.multiple_of(j * SUB, SUB), SUB)
            x = cells[:, span, :] + row_b[...]
            x = x.reshape(blocks, block_tiles, SUB, LANES)
            places = [jnp.full((SUB, LANES), place(b), jnp.int32) for b in range(blocks)]
            tops = [jnp.max(x[b], axis=0) for b in range(blocks)]
            peaks = []
            for w in range(3):
                held = [jnp.where(places[b] == w, tops[b], LOWEST) for b in range(blocks)]
                peaks.append(functools.reduce(jnp.maximum, held))
            sums = []
            for b in range(blocks):
                top = jnp.where(
                    places[b] == 0, peaks[0], jnp.where(places[b] == 1, peaks[1], peaks[2])
                )
                sums.append(jnp.sum(jnp.exp2(x[b] - top[None]), axis=0))
            for w in range(3):
                held = [jnp.where(places[b] == w, sums[b], 0.0) for b in range(blocks)]
                peak[w, span, :] = peaks[w]
                total[w, span, :] = functools.reduce(jnp.add, held)
            return carry

        lax.fori_loop(0, size // SUB, some_cols, 0)
        m = jnp.max(peak[...], axis=2, keepdims=True)
        s = jnp.sum(total[...] * jnp.exp2(peak[...] - m), axis=2, keepdims=True)
        mine = to_lanes(jnp.broadcast_to(m, peak.shape)) + jnp.log2(
            to_lanes(jnp.broadcast_to(s, total.shape))
        )
        col_src[r] = mine
        copies = [
            remote(
                col_src.at[r, pl.ds(start, count)],
                there.at[r],
                col_send.at[r, slot],
                col_recv.at[r, slot],
                dp_at(step),
                code,
            )
            for slot, (step, start, count, there) in enumerate(
                ((-2, 0, 1, col_r2), (2, 2, 1, col_l2), (-1, 0, 2, col_r1), (1, 1, 2, col_l1))
            )
        ]
        for copy in copies:
            copy.start()
        for copy in copies:
            copy.wait_recv()
        l1, r1 = col_l1[r], col_r1[r]
        sets = (
            (col_l2[r, 0], l1[0], mine[0]),
            (l1[1], mine[1], r1[0]),
            (mine[2], r1[1], col_r2[r, 0]),
        )
        for w, terms in enumerate(sets):
            m = functools.reduce(jnp.maximum, terms)
            s = functools.reduce(jnp.add, [jnp.exp2(term - m) for term in terms])
            value = target - (m + jnp.log2(s))
            for h in range(halves):
                col_b[w, h * LANES : (h + 1) * LANES, :] = to_column(value[h : h + 1])
        for copy in copies:
            copy.wait_send()

    target = math.log2((rows * n_dp) / (size * n_dp * n_code))

    def sweep(r, carry):
        row_update(r)
        col_update(r, target)
        return carry

    lax.fori_loop(0, ROUNDS, sweep, 0)
    row_update(ROUNDS)

    pack = 2 * SUB

    def weigh(j, carry):
        span = pl.ds(pl.multiple_of(j * pack, pack), pack)
        sums = [jnp.zeros((2, SUB, LANES), jnp.float32) for w in range(3)]
        for b in range(blocks):
            at = place(b)
            at_b = jnp.full((2, SUB, LANES), at, jnp.int32)
            g = col_b[at, span, :].reshape(2, SUB, LANES)
            here = jnp.zeros((2, SUB, LANES), jnp.float32)
            for t in range(block_tiles):
                d = b * block_tiles + t
                x = cells[d, span, :].reshape(2, SUB, LANES) + row_b[d][None] + g
                value = jnp.exp2(x)
                here = here + value
                for w in range(3):
                    kept = jnp.where(at_b == w, value, 0.0).reshape(pack, LANES)
                    weight[w, span, d * LANES : (d + 1) * LANES] = kept.astype(jnp.bfloat16)
            for w in range(3):
                sums[w] = sums[w] + jnp.where(at_b == w, here, 0.0)
        for w in range(3):
            total[w, span, :] = sums[w].reshape(pack, LANES)
        return carry

    lax.fori_loop(0, size // pack, weigh, 0)

    mass = jnp.sum(total[...], axis=2, keepdims=True)
    mass = to_lanes(jnp.broadcast_to(mass, total.shape))
    mass_src[...] = mass.astype(jnp.bfloat16).astype(jnp.float32)
    mass_copies = [
        remote(
            mass_src.at[pl.ds(2 * s, 1)],
            mass_in.at[1 - s],
            mass_send.at[s],
            mass_recv.at[1 - s],
            dp_at(2 * s - 1),
            code,
        )
        for s in range(2)
    ]
    for copy in mass_copies:
        copy.start()

    def columns(n):
        return pl.ds(pl.multiple_of(n * piece, piece), piece)

    def numerator(w, n):
        return jnp.dot(weight[w], feat[:, columns(n)], preferred_element_type=jnp.float32)

    def num_copy(s, n):
        w = side(s)
        return remote(
            num_src.at[s, n],
            num_in.at[1 - w // 2, n],
            num_send.at[s, n],
            num_recv.at[1 - w // 2, n],
            dp_at(w - 1),
            code,
        )

    def give(q, carry):
        s, n = q // PIECES, lax.rem(q, PIECES)
        num_src[s, n] = numerator(side(s), n).astype(jnp.bfloat16)
        num_copy(s, n).start()
        return carry

    lax.fori_loop(0, 2 * PIECES, give, 0)

    def keep(n, carry):
        num_own[n] = numerator(1, n).astype(jnp.bfloat16).astype(jnp.float32)
        return carry

    lax.fori_loop(0, PIECES, keep, 0)

    for s in range(2):
        remote(
            mass_src.at[pl.ds(0, 1)], mass_in.at[s], mass_send.at[s], mass_recv.at[s], dp, code
        ).wait_recv()
    for copy in mass_copies:
        copy.wait_send()
    mass_ref[...] = mass_in[0, 0] + mass_src[1] + mass_in[1, 0]

    def finish(n, carry):
        for s in range(2):
            remote(
                num_src.at[s, n], num_in.at[s, n], num_send.at[s, n], num_recv.at[s, n], dp, code
            ).wait()
        whole_ref[n] = (
            num_in[0, n].astype(jnp.float32) + num_own[n] + num_in[1, n].astype(jnp.float32)
        )
        return carry

    lax.fori_loop(0, PIECES, finish, 0)


def divide(whole_ref, mass_in_ref, out_ref, mass_ref):
    size, piece = whole_ref.shape[1], whole_ref.shape[2]
    eye = lax.broadcasted_iota(jnp.int32, (LANES, LANES), 0) == lax.broadcasted_iota(
        jnp.int32, (LANES, LANES), 1
    )
    mass_ref[...] = mass_in_ref[...]
    for h in range(size // LANES):
        row = jnp.broadcast_to(mass_in_ref[h : h + 1, :], (LANES, LANES))
        column = jnp.sum(jnp.where(eye, row, 0.0), axis=1, keepdims=True)
        span = slice(h * LANES, (h + 1) * LANES)
        for n in range(PIECES):
            value = whole_ref[n, span, :] / column
            out_ref[span, n * piece : (n + 1) * piece] = value.astype(out_ref.dtype)


def solution(mesh):
    n_dp, n_code = mesh.shape["dp"], mesh.shape["code"]

    def local(features, centroids, block_lists):
        rows, width = features.shape
        size = centroids.shape[0]
        tiles = rows // LANES
        blocks = block_lists.shape[0]
        block_tiles = tiles // blocks
        halves = size // LANES
        piece = width // PIECES
        updates = ROUNDS + 1
        f32, bf16 = jnp.float32, jnp.bfloat16
        dma = pltpu.SemaphoreType.DMA
        whole, mass = pl.pallas_call(
            functools.partial(kernel, n_dp, n_code),
            out_shape=(
                jax.ShapeDtypeStruct((PIECES, size, piece), f32),
                jax.ShapeDtypeStruct((halves, LANES), f32),
            ),
            in_specs=[
                pl.BlockSpec(memory_space=pltpu.SMEM),
                pl.BlockSpec(memory_space=pl.ANY),
                pl.BlockSpec(memory_space=pl.ANY),
            ],
            out_specs=(
                pl.BlockSpec(memory_space=pltpu.VMEM),
                pl.BlockSpec(memory_space=pltpu.VMEM),
            ),
            scratch_shapes=[
                pltpu.VMEM((rows, width), bf16),
                pltpu.VMEM((3, size, width), bf16),
                pltpu.VMEM((tiles, size, LANES), f32),
                pltpu.VMEM((tiles, SUB, LANES), f32),
                pltpu.VMEM((3, size, LANES), f32),
                pltpu.VMEM((3, size, LANES), f32),
                pltpu.VMEM((3, size, LANES), f32),
                pltpu.VMEM((3, size, rows), bf16),
                pltpu.VMEM((updates, blocks, block_tiles, LANES), f32),
                pltpu.VMEM((updates, blocks, block_tiles, LANES), f32),
                pltpu.VMEM((updates, block_tiles, LANES), f32),
                pltpu.VMEM((updates, Z // NEAR, block_tiles, LANES), f32),
                pltpu.VMEM((updates, block_tiles, LANES), f32),
                pltpu.VMEM((updates, blocks, block_tiles, LANES), f32),
                pltpu.VMEM((ROUNDS, 3, halves, LANES), f32),
                pltpu.VMEM((ROUNDS, 1, halves, LANES), f32),
                pltpu.VMEM((ROUNDS, 2, halves, LANES), f32),
                pltpu.VMEM((ROUNDS, 2, halves, LANES), f32),
                pltpu.VMEM((ROUNDS, 1, halves, LANES), f32),
                pltpu.VMEM((3, halves, LANES), f32),
                pltpu.VMEM((2, 1, halves, LANES), f32),
                pltpu.VMEM((2, PIECES, size, piece), bf16),
                pltpu.VMEM((2, PIECES, size, piece), bf16),
                pltpu.VMEM((PIECES, size, piece), f32),
                dma((blocks,)),
                dma,
                dma((2,)),
                dma((2,)),
                dma((updates,)),
                dma((updates,)),
                dma((updates,)),
                dma((updates,)),
                dma((updates,)),
                dma((updates,)),
                dma((ROUNDS, 4)),
                dma((ROUNDS, 4)),
                dma((2,)),
                dma((2,)),
                dma((2, PIECES)),
                dma((2, PIECES)),
            ],
            compiler_params=pltpu.CompilerParams(
                collective_id=0, has_side_effects=True, vmem_limit_bytes=56 * 1024 * 1024
            ),
            cost_estimate=pl.CostEstimate(
                flops=8 * rows * size * width,
                bytes_accessed=2 * (rows + 2 * size) * width,
                transcendentals=8 * rows * size,
            ),
            name="balanced_kmeans",
        )(block_lists, features, centroids)
        new_centroids, mass = pl.pallas_call(
            divide,
            out_shape=(
                jax.ShapeDtypeStruct((size, width), bf16),
                jax.ShapeDtypeStruct((halves, LANES), f32),
            ),
            cost_estimate=pl.CostEstimate(
                flops=size * width, bytes_accessed=6 * size * width, transcendentals=0
            ),
            name="divide",
        )(whole, mass)
        return new_centroids, mass.reshape(size)

    return jax.shard_map(
        local,
        mesh=mesh,
        in_specs=(P("dp", None), P(("code", "dp"), None), P("dp", None)),
        out_specs=(P(("code", "dp"), None), P(("code", "dp"))),
        check_vma=False,
    )
```

```python
import functools
import math

import jax
import jax.numpy as jnp
from jax import lax
from jax.experimental import pallas as pl
from jax.experimental.pallas import tpu as pltpu
from jax.sharding import PartitionSpec as P

ROUNDS = 3
SOFTMAX_TEMP = 12.0
LOG2E = math.log2(math.e)
LOWEST = -3.0e38
LANES = 128
SUB = 8
PIECES = 3
Z = 16
NEAR = 4
MESH = pl.DeviceIdType.MESH


def kernel(
    n_dp,
    n_code,
    lists_ref,
    feat_hbm,
    cent_hbm,
    whole_ref,
    mass_ref,
    feat,
    win,
    cells,
    row_b,
    col_b,
    peak,
    total,
    weight,
    places,
    lse_src,
    lse_in,
    mid_src,
    mid_in,
    row_src,
    row_in,
    col_src,
    col_l2,
    col_l1,
    col_r1,
    col_r2,
    mass_src,
    mass_in,
    num_src,
    num_in,
    num_sum,
    feat_sem,
    own_sem,
    halo_send,
    halo_recv,
    lse_send,
    lse_recv,
    mid_send,
    mid_recv,
    row_send,
    row_recv,
    col_send,
    col_recv,
    mass_send,
    mass_recv,
    num_send,
    num_recv,
):
    dp = lax.axis_index("dp")
    code = lax.axis_index("code")
    blocks = lists_ref.shape[0]
    rows = feat.shape[0]
    block_rows = rows // blocks
    block_tiles = block_rows // LANES
    tiles = rows // LANES
    size, width = win.shape[1], win.shape[2]
    halves = size // LANES
    piece = width // PIECES
    odd = lax.rem(dp, 2)
    dp_near = {step: lax.rem(dp + (n_dp + step), n_dp) for step in (-2, -1, 1, 2)}
    for b in range(blocks):
        places[b] = jnp.minimum(lax.rem(lists_ref[b, code] + (n_dp + 1) - dp, n_dp), 2)

    y_hi, z = lax.div(code, Z), lax.rem(code, Z)
    quarter, near = lax.div(z, NEAR), lax.rem(z, NEAR)
    quarters, shares = Z // NEAR, NEAR * (n_code // Z)
    share = y_hi * NEAR + near
    mates = []
    for step in range(1, shares):
        other = lax.rem(share + step, shares)
        at = lax.div(other, NEAR) * Z + quarter * NEAR + lax.rem(other, NEAR)
        mates.append((other, at))
    far_mates = []
    for step in range(1, quarters):
        far_mates.append(y_hi * Z + lax.rem(quarter + step, quarters) * NEAR + near)

    def feat_copy(b):
        span = pl.ds(b * block_rows, block_rows)
        return pltpu.make_async_copy(feat_hbm.at[span], feat.at[span], feat_sem.at[b])

    def remote(src, dst, send, recv, to_dp, to_code):
        return pltpu.make_async_remote_copy(
            src_ref=src,
            dst_ref=dst,
            send_sem=send,
            recv_sem=recv,
            device_id=(to_dp, to_code),
            device_id_type=MESH,
        )

    own_copy = pltpu.make_async_copy(cent_hbm, win.at[1], own_sem)
    own_copy.start()
    for b in range(blocks):
        feat_copy(b).start()

    barrier = pltpu.get_barrier_semaphore()
    for step in (-1, 1, -2, 2):
        pl.semaphore_signal(
            barrier, inc=1, device_id=(dp_near[step], code), device_id_type=MESH
        )
    for to in [at for _, at in mates] + far_mates:
        pl.semaphore_signal(barrier, inc=1, device_id=(dp, to), device_id_type=MESH)
    pl.semaphore_wait(barrier, 4 + shares - 1 + quarters - 1)

    ups = (odd, 1 - odd)
    sides = [dp_near[-1] + up * (dp_near[1] - dp_near[-1]) for up in ups]

    def halo(s):
        land = 1 - ups[s]
        return remote(
            cent_hbm, win.at[2 * land], halo_send.at[s], halo_recv.at[land], sides[s], code
        )

    halo(0).start()
    halo(1).start()

    def norms(w):
        wide = win[w].astype(jnp.float32)
        norm = jnp.sum(wide * wide, axis=1, keepdims=True)
        col_b[w] = jnp.broadcast_to(norm * (-LOG2E / SOFTMAX_TEMP), (size, LANES))

    own_copy.wait()
    norms(1)
    for s in range(2):
        halo(s).wait_send()
    for s in range(2):
        remote(cent_hbm, win.at[2 * s], halo_send.at[s], halo_recv.at[s], dp, code).wait_recv()

    eye = lax.broadcasted_iota(jnp.int32, (LANES, LANES), 0) == lax.broadcasted_iota(
        jnp.int32, (LANES, LANES), 1
    )

    def to_lanes(column):
        square = column.reshape(3 * halves, LANES, LANES)
        flat = jnp.sum(jnp.where(eye[None], square, 0.0), axis=1)
        return flat.reshape(3, halves, LANES)

    def to_column(row):
        square = jnp.where(eye, jnp.broadcast_to(row, (LANES, LANES)), 0.0)
        return jnp.broadcast_to(jnp.sum(square, axis=1, keepdims=True), (LANES, LANES))

    def score(b, carry):
        feat_copy(b).wait()
        inner = lax.dot_general(
            win[places[b]],
            feat[pl.ds(pl.multiple_of(b * block_rows, block_rows), block_rows), :],
            (((1,), (1,)), ((), ())),
            preferred_element_type=jnp.float32,
        )
        scaled = inner.astype(jnp.bfloat16).astype(jnp.float32) * (2.0 * LOG2E / SOFTMAX_TEMP)
        for t in range(block_tiles):
            cells[b * block_tiles + t] = scaled[:, t * LANES : (t + 1) * LANES]
        return carry

    lax.fori_loop(0, blocks, score, 0)
    norms(0)
    norms(2)

    def row_block(r, b):
        bias = col_b[places[b]]
        for t in range(block_tiles):
            x = (cells[b * block_tiles + t] + bias).reshape(size // SUB, SUB, LANES)
            m8 = jnp.max(x, axis=0)
            s8 = jnp.sum(jnp.exp2(x - m8[None]), axis=0)
            m = jnp.max(m8, axis=0, keepdims=True)
            s = jnp.sum(s8 * jnp.exp2(m8 - m), axis=0, keepdims=True)
            lse_src[r, b, t : t + 1, :] = m + jnp.log2(s)

    def join(parts):
        m = jnp.max(parts, axis=0)
        return m + jnp.log2(jnp.sum(jnp.exp2(parts - m[None]), axis=0))

    def row_update(r):
        def two_blocks(step, carry):
            row_block(r, 2 * step)
            row_block(r, 2 * step + 1)
            return carry

        lax.fori_loop(0, blocks // 2, two_blocks, 0)
        for b, to in mates:
            remote(
                lse_src.at[r, b], lse_in.at[r, share], lse_send.at[r], lse_recv.at[r], dp, to
            ).start()
        lse_in[r, share] = lse_src[r, share]
        others = pl.ds(0, shares - 1)
        first = remote(
            lse_src.at[r, others], lse_in.at[r, others], lse_send.at[r], lse_recv.at[r], dp, code
        )
        first.wait_recv()
        value = join(lse_in[r])
        mid_src[r] = value
        for to in far_mates:
            remote(
                mid_src.at[r], mid_in.at[r, quarter], mid_send.at[r], mid_recv.at[r], dp, to
            ).start()
        mid_in[r, quarter] = value
        some = pl.ds(0, quarters - 1)
        second = remote(
            mid_in.at[r, some], mid_in.at[r, some], mid_send.at[r], mid_recv.at[r], dp, code
        )
        second.wait_recv()
        value = -join(mid_in[r])
        row_src[r] = value
        for _, to in mates:
            remote(
                row_src.at[r], row_in.at[r, share], row_send.at[r], row_recv.at[r], dp, to
            ).start()
        row_in[r, share] = value
        first.wait_send()
        second.wait_send()
        third = remote(
            row_in.at[r, others], row_in.at[r, others], row_send.at[r], row_recv.at[r], dp, code
        )
        third.wait_recv()
        for b in range(blocks):
            for t in range(block_tiles):
                row_b[b * block_tiles + t] = jnp.broadcast_to(
                    row_in[r, b, t : t + 1, :], (SUB, LANES)
                )
        third.wait_send()

    def col_update(r, target):
        def one_tile(j):
            span = pl.ds(pl.multiple_of(j * SUB, SUB), SUB)
            x = cells[:, span, :] + row_b[...]
            x = x.reshape(blocks, block_tiles, SUB, LANES)
            at = [jnp.full((SUB, LANES), places[b], jnp.int32) for b in range(blocks)]
            tops = [jnp.max(x[b], axis=0) for b in range(blocks)]
            peaks = []
            for w in range(3):
                held = [jnp.where(at[b] == w, tops[b], LOWEST) for b in range(blocks)]
                peaks.append(functools.reduce(jnp.maximum, held))
            sums = []
            for b in range(blocks):
                top = jnp.where(at[b] == 0, peaks[0], jnp.where(at[b] == 1, peaks[1], peaks[2]))
                sums.append(jnp.sum(jnp.exp2(x[b] - top[None]), axis=0))
            for w in range(3):
                held = [jnp.where(at[b] == w, sums[b], 0.0) for b in range(blocks)]
                peak[w, span, :] = peaks[w]
                total[w, span, :] = functools.reduce(jnp.add, held)

        def two_tiles(j, carry):
            one_tile(2 * j)
            one_tile(2 * j + 1)
            return carry

        lax.fori_loop(0, size // SUB // 2, two_tiles, 0)
        m = jnp.max(peak[...], axis=2, keepdims=True)
        s = jnp.sum(total[...] * jnp.exp2(peak[...] - m), axis=2, keepdims=True)
        mine = to_lanes(jnp.broadcast_to(m, peak.shape)) + jnp.log2(
            to_lanes(jnp.broadcast_to(s, total.shape))
        )
        col_src[r] = mine
        copies = [
            remote(
                col_src.at[r, pl.ds(start, count)],
                there.at[r],
                col_send.at[r, slot],
                col_recv.at[r, slot],
                dp_near[step],
                code,
            )
            for slot, (step, start, count, there) in enumerate(
                ((-2, 0, 1, col_r2), (2, 2, 1, col_l2), (-1, 0, 2, col_r1), (1, 1, 2, col_l1))
            )
        ]
        for copy in copies:
            copy.start()
        for copy in copies:
            copy.wait_recv()
        l1, r1 = col_l1[r], col_r1[r]
        sets = (
            (col_l2[r, 0], l1[0], mine[0]),
            (l1[1], mine[1], r1[0]),
            (mine[2], r1[1], col_r2[r, 0]),
        )
        for w, terms in enumerate(sets):
            m = functools.reduce(jnp.maximum, terms)
            s = functools.reduce(jnp.add, [jnp.exp2(term - m) for term in terms])
            value = target - (m + jnp.log2(s))
            for h in range(halves):
                col_b[w, h * LANES : (h + 1) * LANES, :] = to_column(value[h : h + 1])
        for copy in copies:
            copy.wait_send()

    target = math.log2((rows * n_dp) / (size * n_dp * n_code))

    def sweep(r, carry):
        row_update(r)
        col_update(r, target)
        return carry

    lax.fori_loop(0, ROUNDS, sweep, 0)
    row_update(ROUNDS)

    pack = 2 * SUB

    def weigh(j, carry):
        span = pl.ds(pl.multiple_of(j * pack, pack), pack)
        sums = [jnp.zeros((2, SUB, LANES), jnp.float32) for w in range(3)]
        for b in range(blocks):
            g = col_b[places[b], span, :].reshape(2, SUB, LANES)
            here = jnp.zeros((2, SUB, LANES), jnp.float32)
            for t in range(block_tiles):
                d = b * block_tiles + t
                x = cells[d, span, :].reshape(2, SUB, LANES) + row_b[d][None] + g
                value = jnp.exp2(x)
                here = here + value
                low = value.reshape(pack, LANES).astype(jnp.bfloat16)
                weight[b, span, t * LANES : (t + 1) * LANES] = low
            at = jnp.full((2, SUB, LANES), places[b], jnp.int32)
            for w in range(3):
                sums[w] = sums[w] + jnp.where(at == w, here, 0.0)
        for w in range(3):
            total[w, span, :] = sums[w].reshape(pack, LANES)
        return carry

    lax.fori_loop(0, size // pack, weigh, 0)

    mass = jnp.sum(total[...], axis=2, keepdims=True)
    mass = to_lanes(jnp.broadcast_to(mass, total.shape))
    mass_src[...] = mass.astype(jnp.bfloat16).astype(jnp.float32)
    mass_copies = [
        remote(
            mass_src.at[pl.ds(2 * s, 1)],
            mass_in.at[1 - s],
            mass_send.at[s],
            mass_recv.at[1 - s],
            dp_near[2 * s - 1],
            code,
        )
        for s in range(2)
    ]
    for copy in mass_copies:
        copy.start()

    def columns(n):
        return pl.ds(pl.multiple_of(n * piece, piece), piece)

    def num_copy(s, n):
        land = 1 - ups[s]
        return remote(
            num_src.at[s, n],
            num_in.at[land, n],
            num_send.at[s, n],
            num_recv.at[land, n],
            sides[s],
            code,
        )

    def numerators(n, carry):
        for w in range(3):
            num_sum[n, w] = jnp.zeros((size, piece), jnp.float32)

        def two_blocks(step, carry):
            products = []
            for b in (2 * step, 2 * step + 1):
                span = pl.ds(pl.multiple_of(b * block_rows, block_rows), block_rows)
                product = jnp.dot(
                    weight[b], feat[span, columns(n)], preferred_element_type=jnp.float32
                )
                products.append((jnp.full(product.shape, places[b], jnp.int32), product))
            for w in range(3):
                held = [jnp.where(at == w, product, 0.0) for at, product in products]
                num_sum[n, w] = num_sum[n, w] + (held[0] + held[1])
            return carry

        lax.fori_loop(0, blocks // 2, two_blocks, 0)
        for s in range(2):
            num_src[s, n] = num_sum[n, 2 * ups[s]].astype(jnp.bfloat16)
            num_copy(s, n).start()
        return carry

    lax.fori_loop(0, PIECES, numerators, 0)

    for s in range(2):
        remote(
            mass_src.at[pl.ds(0, 1)], mass_in.at[s], mass_send.at[s], mass_recv.at[s], dp, code
        ).wait_recv()
    for copy in mass_copies:
        copy.wait_send()
    mass_ref[...] = mass_in[0, 0] + mass_src[1] + mass_in[1, 0]

    def finish(n, carry):
        for s in range(2):
            remote(
                num_src.at[s, n], num_in.at[s, n], num_send.at[s, n], num_recv.at[s, n], dp, code
            ).wait()
        own = num_sum[n, 1].astype(jnp.bfloat16).astype(jnp.float32)
        whole_ref[n] = (
            num_in[0, n].astype(jnp.float32) + own + num_in[1, n].astype(jnp.float32)
        )
        return carry

    lax.fori_loop(0, PIECES, finish, 0)


def divide(whole_ref, mass_in_ref, out_ref, mass_ref):
    size, piece = whole_ref.shape[1], whole_ref.shape[2]
    eye = lax.broadcasted_iota(jnp.int32, (LANES, LANES), 0) == lax.broadcasted_iota(
        jnp.int32, (LANES, LANES), 1
    )
    mass_ref[...] = mass_in_ref[...]
    for h in range(size // LANES):
        row = jnp.broadcast_to(mass_in_ref[h : h + 1, :], (LANES, LANES))
        column = jnp.sum(jnp.where(eye, row, 0.0), axis=1, keepdims=True)
        span = slice(h * LANES, (h + 1) * LANES)
        for n in range(PIECES):
            value = whole_ref[n, span, :] / column
            out_ref[span, n * piece : (n + 1) * piece] = value.astype(out_ref.dtype)


def solution(mesh):
    n_dp, n_code = mesh.shape["dp"], mesh.shape["code"]

    def local(features, centroids, block_lists):
        rows, width = features.shape
        size = centroids.shape[0]
        tiles = rows // LANES
        blocks = block_lists.shape[0]
        block_tiles = tiles // blocks
        halves = size // LANES
        piece = width // PIECES
        updates = ROUNDS + 1
        f32, bf16 = jnp.float32, jnp.bfloat16
        dma = pltpu.SemaphoreType.DMA
        whole, mass = pl.pallas_call(
            functools.partial(kernel, n_dp, n_code),
            out_shape=(
                jax.ShapeDtypeStruct((PIECES, size, piece), f32),
                jax.ShapeDtypeStruct((halves, LANES), f32),
            ),
            in_specs=[
                pl.BlockSpec(memory_space=pltpu.SMEM),
                pl.BlockSpec(memory_space=pl.ANY),
                pl.BlockSpec(memory_space=pl.ANY),
            ],
            out_specs=(
                pl.BlockSpec(memory_space=pltpu.VMEM),
                pl.BlockSpec(memory_space=pltpu.VMEM),
            ),
            scratch_shapes=[
                pltpu.VMEM((rows, width), bf16),
                pltpu.VMEM((3, size, width), bf16),
                pltpu.VMEM((tiles, size, LANES), f32),
                pltpu.VMEM((tiles, SUB, LANES), f32),
                pltpu.VMEM((3, size, LANES), f32),
                pltpu.VMEM((3, size, LANES), f32),
                pltpu.VMEM((3, size, LANES), f32),
                pltpu.VMEM((blocks, size, rows // blocks), bf16),
                pltpu.SMEM((blocks,), jnp.int32),
                pltpu.VMEM((updates, blocks, block_tiles, LANES), f32),
                pltpu.VMEM((updates, blocks, block_tiles, LANES), f32),
                pltpu.VMEM((updates, block_tiles, LANES), f32),
                pltpu.VMEM((updates, Z // NEAR, block_tiles, LANES), f32),
                pltpu.VMEM((updates, block_tiles, LANES), f32),
                pltpu.VMEM((updates, blocks, block_tiles, LANES), f32),
                pltpu.VMEM((ROUNDS, 3, halves, LANES), f32),
                pltpu.VMEM((ROUNDS, 1, halves, LANES), f32),
                pltpu.VMEM((ROUNDS, 2, halves, LANES), f32),
                pltpu.VMEM((ROUNDS, 2, halves, LANES), f32),
                pltpu.VMEM((ROUNDS, 1, halves, LANES), f32),
                pltpu.VMEM((3, halves, LANES), f32),
                pltpu.VMEM((2, 1, halves, LANES), f32),
                pltpu.VMEM((2, PIECES, size, piece), bf16),
                pltpu.VMEM((2, PIECES, size, piece), bf16),
                pltpu.VMEM((PIECES, 3, size, piece), f32),
                dma((blocks,)),
                dma,
                dma((2,)),
                dma((2,)),
                dma((updates,)),
                dma((updates,)),
                dma((updates,)),
                dma((updates,)),
                dma((updates,)),
                dma((updates,)),
                dma((ROUNDS, 4)),
                dma((ROUNDS, 4)),
                dma((2,)),
                dma((2,)),
                dma((2, PIECES)),
                dma((2, PIECES)),
            ],
            compiler_params=pltpu.CompilerParams(
                collective_id=0, has_side_effects=True, vmem_limit_bytes=56 * 1024 * 1024
            ),
            cost_estimate=pl.CostEstimate(
                flops=8 * rows * size * width,
                bytes_accessed=2 * (rows + 2 * size) * width,
                transcendentals=8 * rows * size,
            ),
            name="balanced_kmeans",
        )(block_lists, features, centroids)
        new_centroids, mass = pl.pallas_call(
            divide,
            out_shape=(
                jax.ShapeDtypeStruct((size, width), bf16),
                jax.ShapeDtypeStruct((halves, LANES), f32),
            ),
            cost_estimate=pl.CostEstimate(
                flops=size * width, bytes_accessed=6 * size * width, transcendentals=0
            ),
            name="divide",
        )(whole, mass)
        return new_centroids, mass.reshape(size)

    return jax.shard_map(
        local,
        mesh=mesh,
        in_specs=(P("dp", None), P(("code", "dp"), None), P("dp", None)),
        out_specs=(P(("code", "dp"), None), P(("code", "dp"))),
        check_vma=False,
    )
```

```python
import functools
import math

import jax
import jax.numpy as jnp
from jax import lax
from jax.experimental import pallas as pl
from jax.experimental.pallas import tpu as pltpu
from jax.sharding import PartitionSpec as P

ROUNDS = 3
SOFTMAX_TEMP = 12.0
LOG2E = math.log2(math.e)
LOWEST = -3.0e38
LANES = 128
SUB = 8
PIECES = 3
Z = 16
NEAR = 4
MESH = pl.DeviceIdType.MESH


def remote(src, dst, send, recv, to_dp, to_code):
    return pltpu.make_async_remote_copy(
        src_ref=src,
        dst_ref=dst,
        send_sem=send,
        recv_sem=recv,
        device_id=(to_dp, to_code),
        device_id_type=MESH,
    )


def sides_of(n_dp):
    dp = lax.axis_index("dp")
    odd = lax.rem(dp, 2)
    left, right = lax.rem(dp + n_dp - 1, n_dp), lax.rem(dp + 1, n_dp)
    ups = (odd, 1 - odd)
    return ups, [left + up * (right - left) for up in ups]


def greet(partners):
    barrier = pltpu.get_barrier_semaphore()
    for to in partners:
        pl.semaphore_signal(barrier, inc=1, device_id=to, device_id_type=MESH)
    pl.semaphore_wait(barrier, len(partners))


def read_places(n_dp, lists_ref, places):
    dp, code = lax.axis_index("dp"), lax.axis_index("code")
    for b in range(lists_ref.shape[0]):
        places[b] = jnp.minimum(lax.rem(lists_ref[b, code] + (n_dp + 1) - dp, n_dp), 2)


def halo_kernel(n_dp, cent_hbm, win_ref, win, own_sem, send, recv):
    dp, code = lax.axis_index("dp"), lax.axis_index("code")
    own = pltpu.make_async_copy(cent_hbm, win.at[1], own_sem)
    own.start()
    ups, sides = sides_of(n_dp)
    greet([(to, code) for to in sides])
    copies = []
    for s in range(2):
        land = 1 - ups[s]
        copies.append(
            remote(cent_hbm, win.at[2 * land], send.at[s], recv.at[land], sides[s], code)
        )
    for copy in copies:
        copy.start()
    own.wait()
    win_ref[1] = win[1]
    for copy in copies:
        copy.wait_send()
    for s in range(2):
        remote(cent_hbm, win.at[2 * s], send.at[s], recv.at[s], dp, code).wait_recv()
    win_ref[0] = win[0]
    win_ref[2] = win[2]


def score_kernel(n_dp, lists_ref, win_ref, feat_ref, inner_ref, bias_ref, places):
    b = pl.program_id(0)

    @pl.when(b == 0)
    def _():
        read_places(n_dp, lists_ref, places)
        for w in range(3):
            wide = win_ref[w].astype(jnp.float32)
            norm = jnp.sum(wide * wide, axis=1, keepdims=True)
            bias_ref[w] = jnp.broadcast_to(norm * (-LOG2E / SOFTMAX_TEMP), bias_ref.shape[1:])

    inner = lax.dot_general(
        win_ref[places[b]],
        feat_ref[...],
        (((1,), (1,)), ((), ())),
        preferred_element_type=jnp.float32,
    )
    inner_ref[0] = inner.astype(jnp.bfloat16)


def sum_kernel(n_dp, lists_ref, weight_ref, feat_ref, out_ref, total, places):
    b = pl.program_id(0)

    @pl.when(b == 0)
    def _():
        read_places(n_dp, lists_ref, places)
        total[...] = jnp.zeros_like(total)

    w = places[b]
    total[w] = total[w] + jnp.dot(
        weight_ref[0], feat_ref[...], preferred_element_type=jnp.float32
    )

    @pl.when(b == pl.num_programs(0) - 1)
    def _():
        out_ref[...] = total[...].astype(jnp.bfloat16)


def exchange_kernel(n_dp, num_ref, mass_ref, whole_ref, mass_out, num_in, mass_in, send, recv, m_send, m_recv):
    dp, code = lax.axis_index("dp"), lax.axis_index("code")
    ups, sides = sides_of(n_dp)
    greet([(to, code) for to in sides])
    copies = []
    for s in range(2):
        land = 1 - ups[s]
        copies.append(
            remote(
                mass_ref.at[2 * ups[s]], mass_in.at[land], m_send.at[s], m_recv.at[land], sides[s], code
            )
        )
        copies.append(
            remote(num_ref.at[2 * ups[s]], num_in.at[land], send.at[s], recv.at[land], sides[s], code)
        )
    for copy in copies:
        copy.start()
    for copy in copies:
        copy.wait_send()
    for s in range(2):
        remote(mass_ref.at[0], mass_in.at[s], m_send.at[s], m_recv.at[s], dp, code).wait_recv()
        remote(num_ref.at[0], num_in.at[s], send.at[s], recv.at[s], dp, code).wait_recv()
    mass_out[...] = mass_in[0] + mass_ref[1] + mass_in[1]
    whole_ref[...] = (
        num_in[0].astype(jnp.float32)
        + num_ref[1].astype(jnp.float32)
        + num_in[1].astype(jnp.float32)
    )


def scale_kernel(
    n_dp,
    n_code,
    lists_ref,
    inner_ref,
    bias_ref,
    weight,
    mass_ref,
    cells,
    row_b,
    col_b,
    peak,
    total,
    places,
    lse_src,
    lse_in,
    mid_src,
    mid_in,
    row_src,
    row_in,
    col_src,
    col_l2,
    col_l1,
    col_r1,
    col_r2,
    lse_send,
    lse_recv,
    mid_send,
    mid_recv,
    row_send,
    row_recv,
    col_send,
    col_recv,
):
    dp = lax.axis_index("dp")
    code = lax.axis_index("code")
    blocks = lists_ref.shape[0]
    size, block_rows = inner_ref.shape[1], inner_ref.shape[2]
    rows = blocks * block_rows
    block_tiles = block_rows // LANES
    halves = size // LANES
    dp_near = {step: lax.rem(dp + (n_dp + step), n_dp) for step in (-2, -1, 1, 2)}
    read_places(n_dp, lists_ref, places)

    y_hi, z = lax.div(code, Z), lax.rem(code, Z)
    quarter, near = lax.div(z, NEAR), lax.rem(z, NEAR)
    quarters, shares = Z // NEAR, NEAR * (n_code // Z)
    share = y_hi * NEAR + near
    mates = []
    for step in range(1, shares):
        other = lax.rem(share + step, shares)
        at = lax.div(other, NEAR) * Z + quarter * NEAR + lax.rem(other, NEAR)
        mates.append((other, at))
    far_mates = []
    for step in range(1, quarters):
        far_mates.append(y_hi * Z + lax.rem(quarter + step, quarters) * NEAR + near)

    greet(
        [(dp_near[step], code) for step in (-1, 1, -2, 2)]
        + [(dp, at) for _, at in mates]
        + [(dp, at) for at in far_mates]
    )
    col_b[...] = bias_ref[...]

    def unfold(b, carry):
        scaled = inner_ref[b].astype(jnp.float32) * (2.0 * LOG2E / SOFTMAX_TEMP)
        for t in range(block_tiles):
            cells[b * block_tiles + t] = scaled[:, t * LANES : (t + 1) * LANES]
        return carry

    lax.fori_loop(0, blocks, unfold, 0)

    eye = lax.broadcasted_iota(jnp.int32, (LANES, LANES), 0) == lax.broadcasted_iota(
        jnp.int32, (LANES, LANES), 1
    )

    def to_lanes(column):
        square = column.reshape(3 * halves, LANES, LANES)
        flat = jnp.sum(jnp.where(eye[None], square, 0.0), axis=1)
        return flat.reshape(3, halves, LANES)

    def to_column(row):
        square = jnp.where(eye, jnp.broadcast_to(row, (LANES, LANES)), 0.0)
        return jnp.broadcast_to(jnp.sum(square, axis=1, keepdims=True), (LANES, LANES))

    def row_block(r, b):
        bias = col_b[places[b]]
        for t in range(block_tiles):
            x = (cells[b * block_tiles + t] + bias).reshape(size // SUB, SUB, LANES)
            m8 = jnp.max(x, axis=0)
            s8 = jnp.sum(jnp.exp2(x - m8[None]), axis=0)
            m = jnp.max(m8, axis=0, keepdims=True)
            s = jnp.sum(s8 * jnp.exp2(m8 - m), axis=0, keepdims=True)
            lse_src[r, b, t : t + 1, :] = m + jnp.log2(s)

    def join(parts):
        m = jnp.max(parts, axis=0)
        return m + jnp.log2(jnp.sum(jnp.exp2(parts - m[None]), axis=0))

    def row_update(r):
        def two_blocks(step, carry):
            row_block(r, 2 * step)
            row_block(r, 2 * step + 1)
            return carry

        lax.fori_loop(0, blocks // 2, two_blocks, 0)
        for b, to in mates:
            remote(
                lse_src.at[r, b], lse_in.at[r, share], lse_send.at[r], lse_recv.at[r], dp, to
            ).start()
        lse_in[r, share] = lse_src[r, share]
        others = pl.ds(0, shares - 1)
        first = remote(
            lse_src.at[r, others], lse_in.at[r, others], lse_send.at[r], lse_recv.at[r], dp, code
        )
        first.wait_recv()
        value = join(lse_in[r])
        mid_src[r] = value
        for to in far_mates:
            remote(
                mid_src.at[r], mid_in.at[r, quarter], mid_send.at[r], mid_recv.at[r], dp, to
            ).start()
        mid_in[r, quarter] = value
        some = pl.ds(0, quarters - 1)
        second = remote(
            mid_in.at[r, some], mid_in.at[r, some], mid_send.at[r], mid_recv.at[r], dp, code
        )
        second.wait_recv()
        value = -join(mid_in[r])
        row_src[r] = value
        for _, to in mates:
            remote(
                row_src.at[r], row_in.at[r, share], row_send.at[r], row_recv.at[r], dp, to
            ).start()
        row_in[r, share] = value
        first.wait_send()
        second.wait_send()
        third = remote(
            row_in.at[r, others], row_in.at[r, others], row_send.at[r], row_recv.at[r], dp, code
        )
        third.wait_recv()
        for b in range(blocks):
            for t in range(block_tiles):
                row_b[b * block_tiles + t] = jnp.broadcast_to(
                    row_in[r, b, t : t + 1, :], (SUB, LANES)
                )
        third.wait_send()

    def col_update(r, target):
        def one_tile(j):
            span = pl.ds(pl.multiple_of(j * SUB, SUB), SUB)
            x = cells[:, span, :] + row_b[...]
            x = x.reshape(blocks, block_tiles, SUB, LANES)
            at = [jnp.full((SUB, LANES), places[b], jnp.int32) for b in range(blocks)]
            tops = [jnp.max(x[b], axis=0) for b in range(blocks)]
            peaks = []
            for w in range(3):
                held = [jnp.where(at[b] == w, tops[b], LOWEST) for b in range(blocks)]
                peaks.append(functools.reduce(jnp.maximum, held))
            sums = []
            for b in range(blocks):
                top = jnp.where(at[b] == 0, peaks[0], jnp.where(at[b] == 1, peaks[1], peaks[2]))
                sums.append(jnp.sum(jnp.exp2(x[b] - top[None]), axis=0))
            for w in range(3):
                held = [jnp.where(at[b] == w, sums[b], 0.0) for b in range(blocks)]
                peak[w, span, :] = peaks[w]
                total[w, span, :] = functools.reduce(jnp.add, held)

        def two_tiles(j, carry):
            one_tile(2 * j)
            one_tile(2 * j + 1)
            return carry

        lax.fori_loop(0, size // SUB // 2, two_tiles, 0)
        m = jnp.max(peak[...], axis=2, keepdims=True)
        s = jnp.sum(total[...] * jnp.exp2(peak[...] - m), axis=2, keepdims=True)
        mine = to_lanes(jnp.broadcast_to(m, peak.shape)) + jnp.log2(
            to_lanes(jnp.broadcast_to(s, total.shape))
        )
        col_src[r] = mine
        copies = [
            remote(
                col_src.at[r, pl.ds(start, count)],
                there.at[r],
                col_send.at[r, slot],
                col_recv.at[r, slot],
                dp_near[step],
                code,
            )
            for slot, (step, start, count, there) in enumerate(
                ((-2, 0, 1, col_r2), (2, 2, 1, col_l2), (-1, 0, 2, col_r1), (1, 1, 2, col_l1))
            )
        ]
        for copy in copies:
            copy.start()
        for copy in copies:
            copy.wait_recv()
        l1, r1 = col_l1[r], col_r1[r]
        sets = (
            (col_l2[r, 0], l1[0], mine[0]),
            (l1[1], mine[1], r1[0]),
            (mine[2], r1[1], col_r2[r, 0]),
        )
        for w, terms in enumerate(sets):
            m = functools.reduce(jnp.maximum, terms)
            s = functools.reduce(jnp.add, [jnp.exp2(term - m) for term in terms])
            value = target - (m + jnp.log2(s))
            for h in range(halves):
                col_b[w, h * LANES : (h + 1) * LANES, :] = to_column(value[h : h + 1])
        for copy in copies:
            copy.wait_send()

    target = math.log2((rows * n_dp) / (size * n_dp * n_code))

    def sweep(r, carry):
        row_update(r)
        col_update(r, target)
        return carry

    lax.fori_loop(0, ROUNDS, sweep, 0)
    row_update(ROUNDS)

    pack = 2 * SUB

    def weigh(j, carry):
        span = pl.ds(pl.multiple_of(j * pack, pack), pack)
        sums = [jnp.zeros((2, SUB, LANES), jnp.float32) for w in range(3)]
        for b in range(blocks):
            g = col_b[places[b], span, :].reshape(2, SUB, LANES)
            here = jnp.zeros((2, SUB, LANES), jnp.float32)
            for t in range(block_tiles):
                d = b * block_tiles + t
                x = cells[d, span, :].reshape(2, SUB, LANES) + row_b[d][None] + g
                value = jnp.exp2(x)
                here = here + value
                low = value.reshape(pack, LANES).astype(jnp.bfloat16)
                weight[b, span, t * LANES : (t + 1) * LANES] = low
            at = jnp.full((2, SUB, LANES), places[b], jnp.int32)
            for w in range(3):
                sums[w] = sums[w] + jnp.where(at == w, here, 0.0)
        for w in range(3):
            total[w, span, :] = sums[w].reshape(pack, LANES)
        return carry

    lax.fori_loop(0, size // pack, weigh, 0)

    mass = jnp.sum(total[...], axis=2, keepdims=True)
    mass = to_lanes(jnp.broadcast_to(mass, total.shape))
    mass_ref[...] = mass.astype(jnp.bfloat16).astype(jnp.float32)


def divide(whole_ref, mass_in_ref, out_ref, mass_ref):
    size = whole_ref.shape[0]
    eye = lax.broadcasted_iota(jnp.int32, (LANES, LANES), 0) == lax.broadcasted_iota(
        jnp.int32, (LANES, LANES), 1
    )
    mass_ref[...] = mass_in_ref[...]
    for h in range(size // LANES):
        row = jnp.broadcast_to(mass_in_ref[h : h + 1, :], (LANES, LANES))
        column = jnp.sum(jnp.where(eye, row, 0.0), axis=1, keepdims=True)
        span = slice(h * LANES, (h + 1) * LANES)
        out_ref[span, :] = (whole_ref[span, :] / column).astype(out_ref.dtype)


def solution(mesh):
    n_dp, n_code = mesh.shape["dp"], mesh.shape["code"]

    def local(features, centroids, block_lists):
        rows, width = features.shape
        size = centroids.shape[0]
        tiles = rows // LANES
        blocks = block_lists.shape[0]
        block_rows = rows // blocks
        block_tiles = tiles // blocks
        halves = size // LANES
        updates = ROUNDS + 1
        f32, bf16 = jnp.float32, jnp.bfloat16
        dma = pltpu.SemaphoreType.DMA
        shape = jax.ShapeDtypeStruct
        smem = pl.BlockSpec(memory_space=pltpu.SMEM)
        vmem = pl.BlockSpec(memory_space=pltpu.VMEM)
        anywhere = pl.BlockSpec(memory_space=pl.ANY)
        limit = 48 * 1024 * 1024

        def whole_block(*sizes):
            return pl.BlockSpec(sizes, lambda b: (0,) * len(sizes))

        def per_block(*sizes):
            return pl.BlockSpec(sizes, lambda b: (b,) + (0,) * (len(sizes) - 1))

        window = pl.pallas_call(
            functools.partial(halo_kernel, n_dp),
            out_shape=shape((3, size, width), bf16),
            in_specs=[anywhere],
            out_specs=vmem,
            scratch_shapes=[pltpu.VMEM((3, size, width), bf16), dma, dma((2,)), dma((2,))],
            compiler_params=pltpu.CompilerParams(
                collective_id=0, has_side_effects=True, vmem_limit_bytes=limit
            ),
            name="halo",
        )(centroids)
        inner, bias = pl.pallas_call(
            functools.partial(score_kernel, n_dp),
            grid=(blocks,),
            out_shape=(shape((blocks, size, block_rows), bf16), shape((3, size, LANES), f32)),
            in_specs=[smem, whole_block(3, size, width), per_block(block_rows, width)],
            out_specs=(per_block(1, size, block_rows), whole_block(3, size, LANES)),
            scratch_shapes=[pltpu.SMEM((blocks,), jnp.int32)],
            compiler_params=pltpu.CompilerParams(vmem_limit_bytes=limit),
            name="score",
        )(block_lists, window, features)
        weight, mass = pl.pallas_call(
            functools.partial(scale_kernel, n_dp, n_code),
            out_shape=(shape((blocks, size, block_rows), bf16), shape((3, halves, LANES), f32)),
            in_specs=[smem, vmem, vmem],
            out_specs=(vmem, vmem),
            scratch_shapes=[
                pltpu.VMEM((tiles, size, LANES), f32),
                pltpu.VMEM((tiles, SUB, LANES), f32),
                pltpu.VMEM((3, size, LANES), f32),
                pltpu.VMEM((3, size, LANES), f32),
                pltpu.VMEM((3, size, LANES), f32),
                pltpu.SMEM((blocks,), jnp.int32),
                pltpu.VMEM((updates, blocks, block_tiles, LANES), f32),
                pltpu.VMEM((updates, blocks, block_tiles, LANES), f32),
                pltpu.VMEM((updates, block_tiles, LANES), f32),
                pltpu.VMEM((updates, Z // NEAR, block_tiles, LANES), f32),
                pltpu.VMEM((updates, block_tiles, LANES), f32),
                pltpu.VMEM((updates, blocks, block_tiles, LANES), f32),
                pltpu.VMEM((ROUNDS, 3, halves, LANES), f32),
                pltpu.VMEM((ROUNDS, 1, halves, LANES), f32),
                pltpu.VMEM((ROUNDS, 2, halves, LANES), f32),
                pltpu.VMEM((ROUNDS, 2, halves, LANES), f32),
                pltpu.VMEM((ROUNDS, 1, halves, LANES), f32),
                dma((updates,)),
                dma((updates,)),
                dma((updates,)),
                dma((updates,)),
                dma((updates,)),
                dma((updates,)),
                dma((ROUNDS, 4)),
                dma((ROUNDS, 4)),
            ],
            compiler_params=pltpu.CompilerParams(
                collective_id=1, has_side_effects=True, vmem_limit_bytes=limit
            ),
            name="scale",
        )(block_lists, inner, bias)
        partial_sums = pl.pallas_call(
            functools.partial(sum_kernel, n_dp),
            grid=(blocks,),
            out_shape=shape((3, size, width), bf16),
            in_specs=[smem, per_block(1, size, block_rows), per_block(block_rows, width)],
            out_specs=whole_block(3, size, width),
            scratch_shapes=[pltpu.VMEM((3, size, width), f32), pltpu.SMEM((blocks,), jnp.int32)],
            compiler_params=pltpu.CompilerParams(vmem_limit_bytes=limit),
            name="sums",
        )(block_lists, weight, features)
        whole, mass = pl.pallas_call(
            functools.partial(exchange_kernel, n_dp),
            out_shape=(shape((size, width), f32), shape((halves, LANES), f32)),
            in_specs=[vmem, vmem],
            out_specs=(vmem, vmem),
            scratch_shapes=[
                pltpu.VMEM((2, size, width), bf16),
                pltpu.VMEM((2, halves, LANES), f32),
                dma((2,)),
                dma((2,)),
                dma((2,)),
                dma((2,)),
            ],
            compiler_params=pltpu.CompilerParams(
                collective_id=2, has_side_effects=True, vmem_limit_bytes=limit
            ),
            name="exchange",
        )(partial_sums, mass)
        new_centroids, mass = pl.pallas_call(
            divide,
            out_shape=(shape((size, width), bf16), shape((halves, LANES), f32)),
            name="divide",
        )(whole, mass)
        return new_centroids, mass.reshape(size)

    return jax.shard_map(
        local,
        mesh=mesh,
        in_specs=(P("dp", None), P(("code", "dp"), None), P("dp", None)),
        out_specs=(P(("code", "dp"), None), P(("code", "dp"))),
        check_vma=False,
    )
```

```python
import functools
import math

import jax
import jax.numpy as jnp
from jax import lax
from jax.experimental import pallas as pl
from jax.experimental.pallas import tpu as pltpu
from jax.sharding import PartitionSpec as P

ROUNDS = 3
SOFTMAX_TEMP = 12.0
LOG2E = math.log2(math.e)
LOWEST = -3.0e38
LANES = 128
SUB = 8
PIECES = 3
Z = 16
NEAR = 4
MESH = pl.DeviceIdType.MESH


def kernel(
    n_dp,
    n_code,
    lists_ref,
    feat_hbm,
    cent_hbm,
    whole_ref,
    mass_ref,
    feat,
    win,
    cells,
    row_b,
    col_b,
    peak,
    total,
    weight,
    places,
    lse_src,
    lse_in,
    mid_src,
    mid_in,
    row_src,
    row_in,
    col_src,
    col_l2,
    col_l1,
    col_r1,
    col_r2,
    mass_src,
    mass_in,
    num_src,
    num_in,
    num_sum,
    feat_sem,
    own_sem,
    halo_send,
    halo_recv,
    lse_send,
    lse_recv,
    mid_send,
    mid_recv,
    row_send,
    row_recv,
    col_send,
    col_recv,
    mass_send,
    mass_recv,
    num_send,
    num_recv,
):
    dp = lax.axis_index("dp")
    code = lax.axis_index("code")
    blocks = lists_ref.shape[0]
    rows = feat.shape[0]
    block_rows = rows // blocks
    block_tiles = block_rows // LANES
    tiles = rows // LANES
    size, width = win.shape[1], win.shape[2]
    halves = size // LANES
    piece = width // PIECES
    odd = lax.rem(dp, 2)
    dp_near = {step: lax.rem(dp + (n_dp + step), n_dp) for step in (-2, -1, 1, 2)}
    for b in range(blocks):
        places[b] = jnp.minimum(lax.rem(lists_ref[b, code] + (n_dp + 1) - dp, n_dp), 2)

    y_hi, z = lax.div(code, Z), lax.rem(code, Z)
    quarter, near = lax.div(z, NEAR), lax.rem(z, NEAR)
    quarters, shares = Z // NEAR, NEAR * (n_code // Z)
    share = y_hi * NEAR + near
    mates = []
    for step in range(1, shares):
        other = lax.rem(share + step, shares)
        at = lax.div(other, NEAR) * Z + quarter * NEAR + lax.rem(other, NEAR)
        mates.append((other, at))
    owners = [(b // NEAR) * Z + quarter * NEAR + b % NEAR for b in range(shares)]
    far_mates = []
    for step in range(1, quarters):
        far_mates.append(y_hi * Z + lax.rem(quarter + step, quarters) * NEAR + near)

    def feat_copy(b):
        span = pl.ds(b * block_rows, block_rows)
        return pltpu.make_async_copy(feat_hbm.at[span], feat.at[span], feat_sem.at[b])

    def remote(src, dst, send, recv, to_dp, to_code):
        return pltpu.make_async_remote_copy(
            src_ref=src,
            dst_ref=dst,
            send_sem=send,
            recv_sem=recv,
            device_id=(to_dp, to_code),
            device_id_type=MESH,
        )

    own_copy = pltpu.make_async_copy(cent_hbm, win.at[1], own_sem)
    own_copy.start()
    for b in range(blocks):
        feat_copy(b).start()

    barrier = pltpu.get_barrier_semaphore()
    for step in (-1, 1, -2, 2):
        pl.semaphore_signal(
            barrier, inc=1, device_id=(dp_near[step], code), device_id_type=MESH
        )
    for to in [at for _, at in mates] + far_mates:
        pl.semaphore_signal(barrier, inc=1, device_id=(dp, to), device_id_type=MESH)
    pl.semaphore_wait(barrier, 4 + shares - 1 + quarters - 1)

    ups = (odd, 1 - odd)
    sides = [dp_near[-1] + up * (dp_near[1] - dp_near[-1]) for up in ups]

    def halo(s):
        land = 1 - ups[s]
        return remote(
            cent_hbm, win.at[2 * land], halo_send.at[s], halo_recv.at[land], sides[s], code
        )

    halo(0).start()
    halo(1).start()

    def norms(w):
        wide = win[w].astype(jnp.float32)
        norm = jnp.sum(wide * wide, axis=1, keepdims=True)
        col_b[w] = jnp.broadcast_to(norm * (-LOG2E / SOFTMAX_TEMP), (size, LANES))

    own_copy.wait()
    norms(1)
    for s in range(2):
        halo(s).wait_send()
    for s in range(2):
        remote(cent_hbm, win.at[2 * s], halo_send.at[s], halo_recv.at[s], dp, code).wait_recv()

    eye = lax.broadcasted_iota(jnp.int32, (LANES, LANES), 0) == lax.broadcasted_iota(
        jnp.int32, (LANES, LANES), 1
    )

    def to_lanes(column):
        return jnp.sum(jnp.where(eye[None], column, 0.0), axis=1)

    def to_column(row):
        square = jnp.where(eye, jnp.broadcast_to(row, (LANES, LANES)), 0.0)
        return jnp.broadcast_to(jnp.sum(square, axis=1, keepdims=True), (LANES, LANES))

    def score(b, carry):
        feat_copy(b).wait()
        inner = lax.dot_general(
            win[places[b]],
            feat[pl.ds(pl.multiple_of(b * block_rows, block_rows), block_rows), :],
            (((1,), (1,)), ((), ())),
            preferred_element_type=jnp.float32,
        )
        scaled = inner.astype(jnp.bfloat16).astype(jnp.float32) * (2.0 * LOG2E / SOFTMAX_TEMP)
        for t in range(block_tiles):
            cells[b * block_tiles + t] = scaled[:, t * LANES : (t + 1) * LANES]
        return carry

    lax.fori_loop(0, blocks, score, 0)
    norms(0)
    norms(2)

    def row_block(r, b):
        bias = col_b[places[b]]
        for t in range(block_tiles):
            x = (cells[b * block_tiles + t] + bias).reshape(size // SUB, SUB, LANES)
            m8 = jnp.max(x, axis=0)
            s8 = jnp.sum(jnp.exp2(x - m8[None]), axis=0)
            m = jnp.max(m8, axis=0, keepdims=True)
            s = jnp.sum(s8 * jnp.exp2(m8 - m), axis=0, keepdims=True)
            lse_src[r, b, t : t + 1, :] = m + jnp.log2(s)

    def join(parts):
        m = jnp.max(parts, axis=0)
        return m + jnp.log2(jnp.sum(jnp.exp2(parts - m[None]), axis=0))

    def row_update(r):
        for b in range(blocks):
            row_block(r, b)

            @pl.when(share != b)
            def _():
                remote(
                    lse_src.at[r, b],
                    lse_in.at[r, share],
                    lse_send.at[r],
                    lse_recv.at[r],
                    dp,
                    owners[b],
                ).start()

        lse_in[r, share] = lse_src[r, share]
        others = pl.ds(0, shares - 1)
        first = remote(
            lse_src.at[r, others], lse_in.at[r, others], lse_send.at[r], lse_recv.at[r], dp, code
        )
        first.wait_recv()
        value = join(lse_in[r])
        mid_src[r] = value
        for to in far_mates:
            remote(
                mid_src.at[r], mid_in.at[r, quarter], mid_send.at[r], mid_recv.at[r], dp, to
            ).start()
        mid_in[r, quarter] = value
        some = pl.ds(0, quarters - 1)
        second = remote(
            mid_in.at[r, some], mid_in.at[r, some], mid_send.at[r], mid_recv.at[r], dp, code
        )
        second.wait_recv()
        value = -join(mid_in[r])
        row_src[r] = value
        for _, to in mates:
            remote(
                row_src.at[r], row_in.at[r, share], row_send.at[r], row_recv.at[r, share], dp, to
            ).start()
        row_in[r, share] = value

    def row_arrives(r, some):
        for b in some:

            @pl.when(share != b)
            def _():
                remote(
                    row_src.at[r], row_in.at[r, b], row_send.at[r], row_recv.at[r, b], dp, code
                ).wait_recv()

            for t in range(block_tiles):
                row_b[b * block_tiles + t] = jnp.broadcast_to(
                    row_in[r, b, t : t + 1, :], (SUB, LANES)
                )

    def row_sent(r):
        others, some = pl.ds(0, shares - 1), pl.ds(0, quarters - 1)
        remote(
            lse_src.at[r, others], lse_in.at[r, others], lse_send.at[r], lse_recv.at[r], dp, code
        ).wait_send()
        remote(
            mid_in.at[r, some], mid_in.at[r, some], mid_send.at[r], mid_recv.at[r], dp, code
        ).wait_send()
        remote(
            row_in.at[r, others], row_in.at[r, others], row_send.at[r], row_recv.at[r, 0], dp, code
        ).wait_send()

    def col_update(r, target):
        def one_tile(j, some):
            span = pl.ds(pl.multiple_of(j * SUB, SUB), SUB)
            tiles_of = pl.ds(some[0] * block_tiles, len(some) * block_tiles)
            x = cells[tiles_of, span, :] + row_b[tiles_of]
            x = x.reshape(len(some), block_tiles, SUB, LANES)
            at = [jnp.full((SUB, LANES), places[b], jnp.int32) for b in some]
            tops = [jnp.max(x[i], axis=0) for i in range(len(some))]
            peaks, olds = [], []
            for w in range(3):
                held = [jnp.where(at[i] == w, tops[i], LOWEST) for i in range(len(some))]
                if some[0] > 0:
                    olds.append(peak[w, span, :])
                    held.append(olds[w])
                peaks.append(functools.reduce(jnp.maximum, held))
            sums = []
            for i in range(len(some)):
                top = jnp.where(at[i] == 0, peaks[0], jnp.where(at[i] == 1, peaks[1], peaks[2]))
                sums.append(jnp.sum(jnp.exp2(x[i] - top[None]), axis=0))
            for w in range(3):
                held = [jnp.where(at[i] == w, sums[i], 0.0) for i in range(len(some))]
                if some[0] > 0:
                    held.append(total[w, span, :] * jnp.exp2(olds[w] - peaks[w]))
                peak[w, span, :] = peaks[w]
                total[w, span, :] = functools.reduce(jnp.add, held)

        def tile_loop(first, last, some):
            def two_tiles(j, carry):
                one_tile(2 * j, some)
                one_tile(2 * j + 1, some)
                return carry

            lax.fori_loop(first // 2, last // 2, two_tiles, 0)

        half_tiles = LANES // SUB
        early, late = range(blocks // 2), range(blocks // 2, blocks)
        row_arrives(r, early)
        tile_loop(0, size // SUB, early)
        row_arrives(r, late)
        mines, copies = [], []
        for h in range(halves):
            tile_loop(h * half_tiles, (h + 1) * half_tiles, late)
            span = slice(h * LANES, (h + 1) * LANES)
            tops, sums = peak[:, span, :], total[:, span, :]
            m = jnp.max(tops, axis=2, keepdims=True)
            s = jnp.sum(sums * jnp.exp2(tops - m), axis=2, keepdims=True)
            mine = to_lanes(jnp.broadcast_to(m, tops.shape)) + jnp.log2(
                to_lanes(jnp.broadcast_to(s, sums.shape))
            )
            mines.append(mine)
            for w in range(3):
                col_src[r, h, w] = mine[w : w + 1]
            for slot, (step, start, count, there) in enumerate(
                ((-2, 0, 1, col_r2), (2, 2, 1, col_l2), (-1, 0, 2, col_r1), (1, 1, 2, col_l1))
            ):
                copies.append(
                    remote(
                        col_src.at[r, h, pl.ds(start, count)],
                        there.at[r, h],
                        col_send.at[r, h, slot],
                        col_recv.at[r, h, slot],
                        dp_near[step],
                        code,
                    )
                )
                copies[-1].start()
        for h in range(halves):
            for copy in copies[4 * h : 4 * h + 4]:
                copy.wait_recv()
            mine, l1, r1 = mines[h], col_l1[r, h], col_r1[r, h]
            sets = (
                (col_l2[r, h, 0], l1[0], mine[0:1]),
                (l1[1], mine[1:2], r1[0]),
                (mine[2:3], r1[1], col_r2[r, h, 0]),
            )
            for w, terms in enumerate(sets):
                m = functools.reduce(jnp.maximum, terms)
                s = functools.reduce(jnp.add, [jnp.exp2(term - m) for term in terms])
                value = target - (m + jnp.log2(s))
                col_b[w, h * LANES : (h + 1) * LANES, :] = to_column(value)
        for copy in copies:
            copy.wait_send()
        row_sent(r)

    target = math.log2((rows * n_dp) / (size * n_dp * n_code))

    def sweep(r, carry):
        row_update(r)
        col_update(r, target)
        return carry

    lax.fori_loop(0, ROUNDS, sweep, 0)
    row_update(ROUNDS)
    row_arrives(ROUNDS, range(blocks))
    row_sent(ROUNDS)

    pack = 2 * SUB

    def weigh(j, carry):
        span = pl.ds(pl.multiple_of(j * pack, pack), pack)
        sums = [jnp.zeros((2, SUB, LANES), jnp.float32) for w in range(3)]
        for b in range(blocks):
            g = col_b[places[b], span, :].reshape(2, SUB, LANES)
            here = jnp.zeros((2, SUB, LANES), jnp.float32)
            for t in range(block_tiles):
                d = b * block_tiles + t
                x = cells[d, span, :].reshape(2, SUB, LANES) + row_b[d][None] + g
                value = jnp.exp2(x)
                here = here + value
                low = value.reshape(pack, LANES).astype(jnp.bfloat16)
                weight[b, span, t * LANES : (t + 1) * LANES] = low
            at = jnp.full((2, SUB, LANES), places[b], jnp.int32)
            for w in range(3):
                sums[w] = sums[w] + jnp.where(at == w, here, 0.0)
        for w in range(3):
            total[w, span, :] = sums[w].reshape(pack, LANES)
        return carry

    lax.fori_loop(0, size // pack, weigh, 0)

    mass = jnp.sum(total[...], axis=2, keepdims=True)
    mass = jnp.broadcast_to(mass, total.shape)
    for h in range(halves):
        part = to_lanes(mass[:, h * LANES : (h + 1) * LANES, :])
        mass_src[:, h, :] = part.astype(jnp.bfloat16).astype(jnp.float32)
    mass_copies = [
        remote(
            mass_src.at[pl.ds(2 * s, 1)],
            mass_in.at[1 - s],
            mass_send.at[s],
            mass_recv.at[1 - s],
            dp_near[2 * s - 1],
            code,
        )
        for s in range(2)
    ]
    for copy in mass_copies:
        copy.start()

    def columns(n):
        return pl.ds(pl.multiple_of(n * piece, piece), piece)

    def num_copy(s, n):
        land = 1 - ups[s]
        return remote(
            num_src.at[s, n],
            num_in.at[land, n],
            num_send.at[s, n],
            num_recv.at[land, n],
            sides[s],
            code,
        )

    def numerators(n, carry):
        for w in range(3):
            num_sum[n, w] = jnp.zeros((size, piece), jnp.float32)

        def two_blocks(step, carry):
            products = []
            for b in (2 * step, 2 * step + 1):
                span = pl.ds(pl.multiple_of(b * block_rows, block_rows), block_rows)
                product = jnp.dot(
                    weight[b], feat[span, columns(n)], preferred_element_type=jnp.float32
                )
                products.append((jnp.full(product.shape, places[b], jnp.int32), product))
            for w in range(3):
                held = [jnp.where(at == w, product, 0.0) for at, product in products]
                num_sum[n, w] = num_sum[n, w] + (held[0] + held[1])
            return carry

        lax.fori_loop(0, blocks // 2, two_blocks, 0)
        for s in range(2):
            num_src[s, n] = num_sum[n, 2 * ups[s]].astype(jnp.bfloat16)
            num_copy(s, n).start()
        return carry

    lax.fori_loop(0, PIECES, numerators, 0)

    for s in range(2):
        remote(
            mass_src.at[pl.ds(0, 1)], mass_in.at[s], mass_send.at[s], mass_recv.at[s], dp, code
        ).wait_recv()
    for copy in mass_copies:
        copy.wait_send()
    mass_ref[...] = mass_in[0, 0] + mass_src[1] + mass_in[1, 0]

    def finish(n, carry):
        for s in range(2):
            remote(
                num_src.at[s, n], num_in.at[s, n], num_send.at[s, n], num_recv.at[s, n], dp, code
            ).wait()
        own = num_sum[n, 1].astype(jnp.bfloat16).astype(jnp.float32)
        whole_ref[n] = (
            num_in[0, n].astype(jnp.float32) + own + num_in[1, n].astype(jnp.float32)
        )
        return carry

    lax.fori_loop(0, PIECES, finish, 0)


def divide(whole_ref, mass_in_ref, out_ref, mass_ref):
    size, piece = whole_ref.shape[1], whole_ref.shape[2]
    eye = lax.broadcasted_iota(jnp.int32, (LANES, LANES), 0) == lax.broadcasted_iota(
        jnp.int32, (LANES, LANES), 1
    )
    mass_ref[...] = mass_in_ref[...]
    for h in range(size // LANES):
        row = jnp.broadcast_to(mass_in_ref[h : h + 1, :], (LANES, LANES))
        column = jnp.sum(jnp.where(eye, row, 0.0), axis=1, keepdims=True)
        span = slice(h * LANES, (h + 1) * LANES)
        for n in range(PIECES):
            value = whole_ref[n, span, :] / column
            out_ref[span, n * piece : (n + 1) * piece] = value.astype(out_ref.dtype)


def solution(mesh):
    n_dp, n_code = mesh.shape["dp"], mesh.shape["code"]

    def local(features, centroids, block_lists):
        rows, width = features.shape
        size = centroids.shape[0]
        tiles = rows // LANES
        blocks = block_lists.shape[0]
        block_tiles = tiles // blocks
        halves = size // LANES
        piece = width // PIECES
        updates = ROUNDS + 1
        f32, bf16 = jnp.float32, jnp.bfloat16
        dma = pltpu.SemaphoreType.DMA
        whole, mass = pl.pallas_call(
            functools.partial(kernel, n_dp, n_code),
            out_shape=(
                jax.ShapeDtypeStruct((PIECES, size, piece), f32),
                jax.ShapeDtypeStruct((halves, LANES), f32),
            ),
            in_specs=[
                pl.BlockSpec(memory_space=pltpu.SMEM),
                pl.BlockSpec(memory_space=pl.ANY),
                pl.BlockSpec(memory_space=pl.ANY),
            ],
            out_specs=(
                pl.BlockSpec(memory_space=pltpu.VMEM),
                pl.BlockSpec(memory_space=pltpu.VMEM),
            ),
            scratch_shapes=[
                pltpu.VMEM((rows, width), bf16),
                pltpu.VMEM((3, size, width), bf16),
                pltpu.VMEM((tiles, size, LANES), f32),
                pltpu.VMEM((tiles, SUB, LANES), f32),
                pltpu.VMEM((3, size, LANES), f32),
                pltpu.VMEM((3, size, LANES), f32),
                pltpu.VMEM((3, size, LANES), f32),
                pltpu.VMEM((blocks, size, rows // blocks), bf16),
                pltpu.SMEM((blocks,), jnp.int32),
                pltpu.VMEM((updates, blocks, block_tiles, LANES), f32),
                pltpu.VMEM((updates, blocks, block_tiles, LANES), f32),
                pltpu.VMEM((updates, block_tiles, LANES), f32),
                pltpu.VMEM((updates, Z // NEAR, block_tiles, LANES), f32),
                pltpu.VMEM((updates, block_tiles, LANES), f32),
                pltpu.VMEM((updates, blocks, block_tiles, LANES), f32),
                pltpu.VMEM((ROUNDS, halves, 3, 1, LANES), f32),
                pltpu.VMEM((ROUNDS, halves, 1, 1, LANES), f32),
                pltpu.VMEM((ROUNDS, halves, 2, 1, LANES), f32),
                pltpu.VMEM((ROUNDS, halves, 2, 1, LANES), f32),
                pltpu.VMEM((ROUNDS, halves, 1, 1, LANES), f32),
                pltpu.VMEM((3, halves, LANES), f32),
                pltpu.VMEM((2, 1, halves, LANES), f32),
                pltpu.VMEM((2, PIECES, size, piece), bf16),
                pltpu.VMEM((2, PIECES, size, piece), bf16),
                pltpu.VMEM((PIECES, 3, size, piece), f32),
                dma((blocks,)),
                dma,
                dma((2,)),
                dma((2,)),
                dma((updates,)),
                dma((updates,)),
                dma((updates,)),
                dma((updates,)),
                dma((updates,)),
                dma((updates, blocks)),
                dma((ROUNDS, halves, 4)),
                dma((ROUNDS, halves, 4)),
                dma((2,)),
                dma((2,)),
                dma((2, PIECES)),
                dma((2, PIECES)),
            ],
            compiler_params=pltpu.CompilerParams(
                collective_id=0, has_side_effects=True, vmem_limit_bytes=56 * 1024 * 1024
            ),
            cost_estimate=pl.CostEstimate(
                flops=8 * rows * size * width,
                bytes_accessed=2 * (rows + 2 * size) * width,
                transcendentals=8 * rows * size,
            ),
            name="balanced_kmeans",
        )(block_lists, features, centroids)
        new_centroids, mass = pl.pallas_call(
            divide,
            out_shape=(
                jax.ShapeDtypeStruct((size, width), bf16),
                jax.ShapeDtypeStruct((halves, LANES), f32),
            ),
            cost_estimate=pl.CostEstimate(
                flops=size * width, bytes_accessed=6 * size * width, transcendentals=0
            ),
            name="divide",
        )(whole, mass)
        return new_centroids, mass.reshape(size)

    return jax.shard_map(
        local,
        mesh=mesh,
        in_specs=(P("dp", None), P(("code", "dp"), None), P("dp", None)),
        out_specs=(P(("code", "dp"), None), P(("code", "dp"))),
        check_vma=False,
    )
```

```python
import functools
import math

import jax
import jax.numpy as jnp
from jax import lax
from jax.experimental import pallas as pl
from jax.experimental.pallas import tpu as pltpu
from jax.sharding import PartitionSpec as P

ROUNDS = 3
SOFTMAX_TEMP = 12.0
LOG2E = math.log2(math.e)
LOWEST = -3.0e38
LANES = 128
SUB = 8
PIECES = 3
Z = 16
NEAR = 2
MESH = pl.DeviceIdType.MESH


def kernel(
    n_dp,
    n_code,
    lists_ref,
    feat_hbm,
    cent_hbm,
    whole_ref,
    mass_ref,
    feat,
    win,
    cells,
    row_b,
    col_b,
    peak,
    total,
    weight,
    places,
    lse_src,
    lse_in,
    mid_src,
    mid_in,
    row_src,
    row_in,
    col_src,
    col_l2,
    col_l1,
    col_r1,
    col_r2,
    mass_src,
    mass_in,
    num_src,
    num_in,
    num_sum,
    feat_sem,
    own_sem,
    halo_send,
    halo_recv,
    lse_send,
    lse_recv,
    mid_send,
    mid_recv,
    row_send,
    row_recv,
    col_send,
    col_recv,
    mass_send,
    mass_recv,
    num_send,
    num_recv,
):
    dp = lax.axis_index("dp")
    code = lax.axis_index("code")
    blocks = lists_ref.shape[0]
    rows = feat.shape[0]
    block_rows = rows // blocks
    block_tiles = block_rows // LANES
    tiles = rows // LANES
    size, width = win.shape[1], win.shape[2]
    halves = size // LANES
    piece = width // PIECES
    odd = lax.rem(dp, 2)
    dp_near = {step: lax.rem(dp + (n_dp + step), n_dp) for step in (-2, -1, 1, 2)}
    for b in range(blocks):
        places[b] = jnp.minimum(lax.rem(lists_ref[b, code] + (n_dp + 1) - dp, n_dp), 2)

    y_hi, z = lax.div(code, Z), lax.rem(code, Z)
    quarter, near = lax.div(z, NEAR), lax.rem(z, NEAR)
    quarters, shares = Z // NEAR, NEAR * (n_code // Z)
    share = y_hi * NEAR + near
    held = blocks // shares
    mates = []
    for step in range(1, shares):
        other = lax.rem(share + step, shares)
        at = lax.div(other, NEAR) * Z + quarter * NEAR + lax.rem(other, NEAR)
        mates.append((other, at))
    owners = [(b // NEAR) * Z + quarter * NEAR + b % NEAR for b in range(shares)]
    far_mates = []
    for step in sorted(range(1, quarters), key=lambda step: abs(2 * step - quarters)):
        far_mates.append(y_hi * Z + lax.rem(quarter + step, quarters) * NEAR + near)

    def feat_copy(b):
        span = pl.ds(b * block_rows, block_rows)
        return pltpu.make_async_copy(feat_hbm.at[span], feat.at[span], feat_sem.at[b])

    def remote(src, dst, send, recv, to_dp, to_code):
        return pltpu.make_async_remote_copy(
            src_ref=src,
            dst_ref=dst,
            send_sem=send,
            recv_sem=recv,
            device_id=(to_dp, to_code),
            device_id_type=MESH,
        )

    own_copy = pltpu.make_async_copy(cent_hbm, win.at[1], own_sem)
    own_copy.start()
    for b in range(blocks):
        feat_copy(b).start()

    barrier = pltpu.get_barrier_semaphore()
    for step in (-1, 1, -2, 2):
        pl.semaphore_signal(
            barrier, inc=1, device_id=(dp_near[step], code), device_id_type=MESH
        )
    for to in [at for _, at in mates] + far_mates:
        pl.semaphore_signal(barrier, inc=1, device_id=(dp, to), device_id_type=MESH)
    pl.semaphore_wait(barrier, 4 + shares - 1 + quarters - 1)

    ups = (odd, 1 - odd)
    sides = [dp_near[-1] + up * (dp_near[1] - dp_near[-1]) for up in ups]

    def halo(s):
        land = 1 - ups[s]
        return remote(
            cent_hbm, win.at[2 * land], halo_send.at[s], halo_recv.at[land], sides[s], code
        )

    halo(0).start()
    halo(1).start()

    def norms(w):
        wide = win[w].astype(jnp.float32)
        norm = jnp.sum(wide * wide, axis=1, keepdims=True)
        col_b[w] = jnp.broadcast_to(norm * (-LOG2E / SOFTMAX_TEMP), (size, LANES))

    own_copy.wait()
    norms(1)
    for s in range(2):
        halo(s).wait_send()
    for s in range(2):
        remote(cent_hbm, win.at[2 * s], halo_send.at[s], halo_recv.at[s], dp, code).wait_recv()

    eye = lax.broadcasted_iota(jnp.int32, (LANES, LANES), 0) == lax.broadcasted_iota(
        jnp.int32, (LANES, LANES), 1
    )

    def to_lanes(column):
        return jnp.sum(jnp.where(eye[None], column, 0.0), axis=1)

    def to_column(row):
        square = jnp.where(eye, jnp.broadcast_to(row, (LANES, LANES)), 0.0)
        return jnp.broadcast_to(jnp.sum(square, axis=1, keepdims=True), (LANES, LANES))

    def score(b, carry):
        feat_copy(b).wait()
        inner = lax.dot_general(
            win[places[b]],
            feat[pl.ds(pl.multiple_of(b * block_rows, block_rows), block_rows), :],
            (((1,), (1,)), ((), ())),
            preferred_element_type=jnp.float32,
        )
        scaled = inner.astype(jnp.bfloat16).astype(jnp.float32) * (2.0 * LOG2E / SOFTMAX_TEMP)
        for t in range(block_tiles):
            cells[b * block_tiles + t] = scaled[:, t * LANES : (t + 1) * LANES]
        return carry

    lax.fori_loop(0, blocks, score, 0)
    norms(0)
    norms(2)

    def row_block(r, owner, i):
        b = owner * held + i
        bias = col_b[places[b]]
        for t in range(block_tiles):
            x = (cells[b * block_tiles + t] + bias).reshape(size // SUB, SUB, LANES)
            m8 = jnp.max(x, axis=0)
            s8 = jnp.sum(jnp.exp2(x - m8[None]), axis=0)
            m = jnp.max(m8, axis=0, keepdims=True)
            s = jnp.sum(s8 * jnp.exp2(m8 - m), axis=0, keepdims=True)
            lse_src[r, owner, i, t : t + 1, :] = m + jnp.log2(s)

    def join(parts):
        m = jnp.max(parts, axis=0)
        return m + jnp.log2(jnp.sum(jnp.exp2(parts - m[None]), axis=0))

    def row_update(r):
        for owner in range(shares):
            for b in range(owner * held, (owner + 1) * held):
                row_block(r, owner, b - owner * held)

            @pl.when(share != owner)
            def _():
                remote(
                    lse_src.at[r, owner],
                    lse_in.at[r, share],
                    lse_send.at[r],
                    lse_recv.at[r],
                    dp,
                    owners[owner],
                ).start()

        lse_in[r, share] = lse_src[r, share]
        others = pl.ds(0, shares - 1)
        first = remote(
            lse_src.at[r, others], lse_in.at[r, others], lse_send.at[r], lse_recv.at[r], dp, code
        )
        first.wait_recv()
        value = join(lse_in[r])
        mid_src[r] = value
        for to in far_mates:
            remote(
                mid_src.at[r], mid_in.at[r, quarter], mid_send.at[r], mid_recv.at[r], dp, to
            ).start()
        mid_in[r, quarter] = value
        some = pl.ds(0, quarters - 1)
        second = remote(
            mid_in.at[r, some], mid_in.at[r, some], mid_send.at[r], mid_recv.at[r], dp, code
        )
        second.wait_recv()
        value = -join(mid_in[r])
        row_src[r] = value
        for _, to in mates:
            remote(
                row_src.at[r], row_in.at[r, share], row_send.at[r], row_recv.at[r, share], dp, to
            ).start()
        row_in[r, share] = value

    def row_arrives(r, some):
        for owner in range(some[0] // held, some[-1] // held + 1):

            @pl.when(share != owner)
            def _():
                remote(
                    row_src.at[r],
                    row_in.at[r, owner],
                    row_send.at[r],
                    row_recv.at[r, owner],
                    dp,
                    code,
                ).wait_recv()

            for i in range(held):
                for t in range(block_tiles):
                    row_b[(owner * held + i) * block_tiles + t] = jnp.broadcast_to(
                        row_in[r, owner, i, t : t + 1, :], (SUB, LANES)
                    )

    def row_sent(r):
        others, some = pl.ds(0, shares - 1), pl.ds(0, quarters - 1)
        remote(
            lse_src.at[r, others], lse_in.at[r, others], lse_send.at[r], lse_recv.at[r], dp, code
        ).wait_send()
        remote(
            mid_in.at[r, some], mid_in.at[r, some], mid_send.at[r], mid_recv.at[r], dp, code
        ).wait_send()
        remote(
            row_in.at[r, others], row_in.at[r, others], row_send.at[r], row_recv.at[r, 0], dp, code
        ).wait_send()

    def col_update(r, target):
        def one_tile(j, some):
            span = pl.ds(pl.multiple_of(j * SUB, SUB), SUB)
            tiles_of = pl.ds(some[0] * block_tiles, len(some) * block_tiles)
            x = cells[tiles_of, span, :] + row_b[tiles_of]
            x = x.reshape(len(some), block_tiles, SUB, LANES)
            at = [jnp.full((SUB, LANES), places[b], jnp.int32) for b in some]
            tops = [jnp.max(x[i], axis=0) for i in range(len(some))]
            peaks, olds = [], []
            for w in range(3):
                kept = [jnp.where(at[i] == w, tops[i], LOWEST) for i in range(len(some))]
                if some[0] > 0:
                    olds.append(peak[w, span, :])
                    kept.append(olds[w])
                peaks.append(functools.reduce(jnp.maximum, kept))
            sums = []
            for i in range(len(some)):
                top = jnp.where(at[i] == 0, peaks[0], jnp.where(at[i] == 1, peaks[1], peaks[2]))
                sums.append(jnp.sum(jnp.exp2(x[i] - top[None]), axis=0))
            for w in range(3):
                kept = [jnp.where(at[i] == w, sums[i], 0.0) for i in range(len(some))]
                if some[0] > 0:
                    kept.append(total[w, span, :] * jnp.exp2(olds[w] - peaks[w]))
                peak[w, span, :] = peaks[w]
                total[w, span, :] = functools.reduce(jnp.add, kept)

        def tile_loop(first, last, some):
            def two_tiles(j, carry):
                one_tile(2 * j, some)
                one_tile(2 * j + 1, some)
                return carry

            lax.fori_loop(first // 2, last // 2, two_tiles, 0)

        half_tiles = LANES // SUB
        early, late = range(blocks // 2), range(blocks // 2, blocks)
        row_arrives(r, early)
        tile_loop(0, size // SUB, early)
        row_arrives(r, late)
        mines, copies = [], []
        for h in range(halves):
            tile_loop(h * half_tiles, (h + 1) * half_tiles, late)
            span = slice(h * LANES, (h + 1) * LANES)
            tops, sums = peak[:, span, :], total[:, span, :]
            m = jnp.max(tops, axis=2, keepdims=True)
            s = jnp.sum(sums * jnp.exp2(tops - m), axis=2, keepdims=True)
            mine = to_lanes(jnp.broadcast_to(m, tops.shape)) + jnp.log2(
                to_lanes(jnp.broadcast_to(s, sums.shape))
            )
            mines.append(mine)
            for w in range(3):
                col_src[r, h, w] = mine[w : w + 1]
            for slot, (step, start, count, there) in enumerate(
                ((-2, 0, 1, col_r2), (2, 2, 1, col_l2), (-1, 0, 2, col_r1), (1, 1, 2, col_l1))
            ):
                copies.append(
                    remote(
                        col_src.at[r, h, pl.ds(start, count)],
                        there.at[r, h],
                        col_send.at[r, h, slot],
                        col_recv.at[r, h, slot],
                        dp_near[step],
                        code,
                    )
                )
                copies[-1].start()
        for h in range(halves):
            for copy in copies[4 * h : 4 * h + 4]:
                copy.wait_recv()
            mine, l1, r1 = mines[h], col_l1[r, h], col_r1[r, h]
            sets = (
                (col_l2[r, h, 0], l1[0], mine[0:1]),
                (l1[1], mine[1:2], r1[0]),
                (mine[2:3], r1[1], col_r2[r, h, 0]),
            )
            for w, terms in enumerate(sets):
                m = functools.reduce(jnp.maximum, terms)
                s = functools.reduce(jnp.add, [jnp.exp2(term - m) for term in terms])
                value = target - (m + jnp.log2(s))
                col_b[w, h * LANES : (h + 1) * LANES, :] = to_column(value)
        for copy in copies:
            copy.wait_send()
        row_sent(r)

    target = math.log2((rows * n_dp) / (size * n_dp * n_code))

    def sweep(r, carry):
        row_update(r)
        col_update(r, target)
        return carry

    lax.fori_loop(0, ROUNDS, sweep, 0)
    row_update(ROUNDS)
    row_arrives(ROUNDS, range(blocks))
    row_sent(ROUNDS)

    pack = 2 * SUB

    def weigh(j, carry):
        span = pl.ds(pl.multiple_of(j * pack, pack), pack)
        sums = [jnp.zeros((2, SUB, LANES), jnp.float32) for w in range(3)]
        for b in range(blocks):
            g = col_b[places[b], span, :].reshape(2, SUB, LANES)
            here = jnp.zeros((2, SUB, LANES), jnp.float32)
            for t in range(block_tiles):
                d = b * block_tiles + t
                x = cells[d, span, :].reshape(2, SUB, LANES) + row_b[d][None] + g
                value = jnp.exp2(x)
                here = here + value
                low = value.reshape(pack, LANES).astype(jnp.bfloat16)
                weight[b, span, t * LANES : (t + 1) * LANES] = low
            at = jnp.full((2, SUB, LANES), places[b], jnp.int32)
            for w in range(3):
                sums[w] = sums[w] + jnp.where(at == w, here, 0.0)
        for w in range(3):
            total[w, span, :] = sums[w].reshape(pack, LANES)
        return carry

    lax.fori_loop(0, size // pack, weigh, 0)

    mass = jnp.sum(total[...], axis=2, keepdims=True)
    mass = jnp.broadcast_to(mass, total.shape)
    for h in range(halves):
        part = to_lanes(mass[:, h * LANES : (h + 1) * LANES, :])
        mass_src[:, h, :] = part.astype(jnp.bfloat16).astype(jnp.float32)
    mass_copies = [
        remote(
            mass_src.at[pl.ds(2 * s, 1)],
            mass_in.at[1 - s],
            mass_send.at[s],
            mass_recv.at[1 - s],
            dp_near[2 * s - 1],
            code,
        )
        for s in range(2)
    ]
    for copy in mass_copies:
        copy.start()

    def columns(n):
        return pl.ds(pl.multiple_of(n * piece, piece), piece)

    def num_copy(s, n):
        land = 1 - ups[s]
        return remote(
            num_src.at[s, n],
            num_in.at[land, n],
            num_send.at[s, n],
            num_recv.at[land, n],
            sides[s],
            code,
        )

    def numerators(n, carry):
        for w in range(3):
            num_sum[n, w] = jnp.zeros((size, piece), jnp.float32)

        def two_blocks(step, carry):
            products = []
            for b in (2 * step, 2 * step + 1):
                span = pl.ds(pl.multiple_of(b * block_rows, block_rows), block_rows)
                product = jnp.dot(
                    weight[b], feat[span, columns(n)], preferred_element_type=jnp.float32
                )
                products.append((jnp.full(product.shape, places[b], jnp.int32), product))
            for w in range(3):
                kept = [jnp.where(at == w, product, 0.0) for at, product in products]
                num_sum[n, w] = num_sum[n, w] + (kept[0] + kept[1])
            return carry

        lax.fori_loop(0, blocks // 2, two_blocks, 0)
        for s in range(2):
            num_src[s, n] = num_sum[n, 2 * ups[s]].astype(jnp.bfloat16)
            num_copy(s, n).start()
        return carry

    lax.fori_loop(0, PIECES, numerators, 0)

    for s in range(2):
        remote(
            mass_src.at[pl.ds(0, 1)], mass_in.at[s], mass_send.at[s], mass_recv.at[s], dp, code
        ).wait_recv()
    for copy in mass_copies:
        copy.wait_send()
    mass_ref[...] = mass_in[0, 0] + mass_src[1] + mass_in[1, 0]

    def finish(n, carry):
        for s in range(2):
            remote(
                num_src.at[s, n], num_in.at[s, n], num_send.at[s, n], num_recv.at[s, n], dp, code
            ).wait()
        own = num_sum[n, 1].astype(jnp.bfloat16).astype(jnp.float32)
        whole_ref[n] = (
            num_in[0, n].astype(jnp.float32) + own + num_in[1, n].astype(jnp.float32)
        )
        return carry

    lax.fori_loop(0, PIECES, finish, 0)


def divide(whole_ref, mass_in_ref, out_ref, mass_ref):
    size, piece = whole_ref.shape[1], whole_ref.shape[2]
    eye = lax.broadcasted_iota(jnp.int32, (LANES, LANES), 0) == lax.broadcasted_iota(
        jnp.int32, (LANES, LANES), 1
    )
    mass_ref[...] = mass_in_ref[...]
    for h in range(size // LANES):
        row = jnp.broadcast_to(mass_in_ref[h : h + 1, :], (LANES, LANES))
        column = jnp.sum(jnp.where(eye, row, 0.0), axis=1, keepdims=True)
        span = slice(h * LANES, (h + 1) * LANES)
        for n in range(PIECES):
            value = whole_ref[n, span, :] / column
            out_ref[span, n * piece : (n + 1) * piece] = value.astype(out_ref.dtype)


def solution(mesh):
    n_dp, n_code = mesh.shape["dp"], mesh.shape["code"]

    def local(features, centroids, block_lists):
        rows, width = features.shape
        size = centroids.shape[0]
        tiles = rows // LANES
        blocks = block_lists.shape[0]
        block_tiles = tiles // blocks
        shares = NEAR * (n_code // Z)
        mine = (blocks // shares, block_tiles, LANES)
        halves = size // LANES
        piece = width // PIECES
        updates = ROUNDS + 1
        f32, bf16 = jnp.float32, jnp.bfloat16
        dma = pltpu.SemaphoreType.DMA
        whole, mass = pl.pallas_call(
            functools.partial(kernel, n_dp, n_code),
            out_shape=(
                jax.ShapeDtypeStruct((PIECES, size, piece), f32),
                jax.ShapeDtypeStruct((halves, LANES), f32),
            ),
            in_specs=[
                pl.BlockSpec(memory_space=pltpu.SMEM),
                pl.BlockSpec(memory_space=pl.ANY),
                pl.BlockSpec(memory_space=pl.ANY),
            ],
            out_specs=(
                pl.BlockSpec(memory_space=pltpu.VMEM),
                pl.BlockSpec(memory_space=pltpu.VMEM),
            ),
            scratch_shapes=[
                pltpu.VMEM((rows, width), bf16),
                pltpu.VMEM((3, size, width), bf16),
                pltpu.VMEM((tiles, size, LANES), f32),
                pltpu.VMEM((tiles, SUB, LANES), f32),
                pltpu.VMEM((3, size, LANES), f32),
                pltpu.VMEM((3, size, LANES), f32),
                pltpu.VMEM((3, size, LANES), f32),
                pltpu.VMEM((blocks, size, rows // blocks), bf16),
                pltpu.SMEM((blocks,), jnp.int32),
                pltpu.VMEM((updates, shares, *mine), f32),
                pltpu.VMEM((updates, shares, *mine), f32),
                pltpu.VMEM((updates, *mine), f32),
                pltpu.VMEM((updates, Z // NEAR, *mine), f32),
                pltpu.VMEM((updates, *mine), f32),
                pltpu.VMEM((updates, shares, *mine), f32),
                pltpu.VMEM((ROUNDS, halves, 3, 1, LANES), f32),
                pltpu.VMEM((ROUNDS, halves, 1, 1, LANES), f32),
                pltpu.VMEM((ROUNDS, halves, 2, 1, LANES), f32),
                pltpu.VMEM((ROUNDS, halves, 2, 1, LANES), f32),
                pltpu.VMEM((ROUNDS, halves, 1, 1, LANES), f32),
                pltpu.VMEM((3, halves, LANES), f32),
                pltpu.VMEM((2, 1, halves, LANES), f32),
                pltpu.VMEM((2, PIECES, size, piece), bf16),
                pltpu.VMEM((2, PIECES, size, piece), bf16),
                pltpu.VMEM((PIECES, 3, size, piece), f32),
                dma((blocks,)),
                dma,
                dma((2,)),
                dma((2,)),
                dma((updates,)),
                dma((updates,)),
                dma((updates,)),
                dma((updates,)),
                dma((updates,)),
                dma((updates, shares)),
                dma((ROUNDS, halves, 4)),
                dma((ROUNDS, halves, 4)),
                dma((2,)),
                dma((2,)),
                dma((2, PIECES)),
                dma((2, PIECES)),
            ],
            compiler_params=pltpu.CompilerParams(
                collective_id=0, has_side_effects=True, vmem_limit_bytes=56 * 1024 * 1024
            ),
            cost_estimate=pl.CostEstimate(
                flops=8 * rows * size * width,
                bytes_accessed=2 * (rows + 2 * size) * width,
                transcendentals=8 * rows * size,
            ),
            name="balanced_kmeans",
        )(block_lists, features, centroids)
        new_centroids, mass = pl.pallas_call(
            divide,
            out_shape=(
                jax.ShapeDtypeStruct((size, width), bf16),
                jax.ShapeDtypeStruct((halves, LANES), f32),
            ),
            cost_estimate=pl.CostEstimate(
                flops=size * width, bytes_accessed=6 * size * width, transcendentals=0
            ),
            name="divide",
        )(whole, mass)
        return new_centroids, mass.reshape(size)

    return jax.shard_map(
        local,
        mesh=mesh,
        in_specs=(P("dp", None), P(("code", "dp"), None), P("dp", None)),
        out_specs=(P(("code", "dp"), None), P(("code", "dp"))),
        check_vma=False,
    )
```

```python
import functools
import math

import jax
import jax.numpy as jnp
from jax import lax
from jax.experimental import pallas as pl
from jax.experimental.pallas import tpu as pltpu
from jax.sharding import PartitionSpec as P

ROUNDS = 3
SOFTMAX_TEMP = 12.0
LOG2E = math.log2(math.e)
LOWEST = -3.0e38
LANES = 128
SUB = 8
PIECES = 3
Z = 16
NEAR = 2
MESH = pl.DeviceIdType.MESH


def kernel(
    n_dp,
    n_code,
    lists_ref,
    feat_hbm,
    cent_hbm,
    out_ref,
    mass_ref,
    feat,
    win_a,
    win_b,
    cells,
    row_b,
    col_b,
    peak,
    total,
    weight,
    places,
    lse_src,
    lse_in,
    mid_src,
    mid_in,
    row_src,
    row_in,
    col_src,
    col_l2,
    col_l1,
    col_r1,
    col_r2,
    mass_src,
    mass_in,
    num_src,
    num_in,
    num_sum,
    feat_sem,
    own_sem,
    halo_send,
    halo_recv,
    lse_send,
    lse_recv,
    mid_send,
    mid_recv,
    row_send,
    row_recv,
    col_send,
    col_recv,
    mass_send,
    mass_recv,
    num_send,
    num_recv,
):
    dp = lax.axis_index("dp")
    code = lax.axis_index("code")
    blocks = lists_ref.shape[0]
    rows = feat.shape[0]
    block_rows = rows // blocks
    block_tiles = block_rows // LANES
    tiles = rows // LANES
    wins = (win_a, win_b)
    halves = len(wins)
    size, width = halves * win_a.shape[1], win_a.shape[2]
    piece = width // PIECES
    odd = lax.rem(dp, 2)
    dp_near = {step: lax.rem(dp + (n_dp + step), n_dp) for step in (-2, -1, 1, 2)}
    for b in range(blocks):
        places[b] = jnp.minimum(lax.rem(lists_ref[b, code] + (n_dp + 1) - dp, n_dp), 2)

    y_hi, z = lax.div(code, Z), lax.rem(code, Z)
    quarter, near = lax.div(z, NEAR), lax.rem(z, NEAR)
    quarters, shares = Z // NEAR, NEAR * (n_code // Z)
    share = y_hi * NEAR + near
    held = blocks // shares
    mates = []
    for step in range(1, shares):
        other = lax.rem(share + step, shares)
        at = lax.div(other, NEAR) * Z + quarter * NEAR + lax.rem(other, NEAR)
        mates.append((other, at))
    owners = [(b // NEAR) * Z + quarter * NEAR + b % NEAR for b in range(shares)]
    far_mates = []
    for step in sorted(range(1, quarters), key=lambda step: abs(2 * step - quarters)):
        far_mates.append(y_hi * Z + lax.rem(quarter + step, quarters) * NEAR + near)

    def feat_copy(b):
        span = pl.ds(b * block_rows, block_rows)
        return pltpu.make_async_copy(feat_hbm.at[span], feat.at[span], feat_sem.at[b])

    def remote(src, dst, send, recv, to_dp, to_code):
        return pltpu.make_async_remote_copy(
            src_ref=src,
            dst_ref=dst,
            send_sem=send,
            recv_sem=recv,
            device_id=(to_dp, to_code),
            device_id_type=MESH,
        )

    def half(h):
        return cent_hbm.at[pl.ds(h * LANES, LANES)]

    own_copies = [
        pltpu.make_async_copy(half(h), wins[h].at[1], own_sem.at[h]) for h in range(halves)
    ]
    for copy in own_copies:
        copy.start()
    for b in range(blocks):
        feat_copy(b).start()

    barrier = pltpu.get_barrier_semaphore()
    for step in (-1, 1, -2, 2):
        pl.semaphore_signal(
            barrier, inc=1, device_id=(dp_near[step], code), device_id_type=MESH
        )
    for to in [at for _, at in mates] + far_mates:
        pl.semaphore_signal(barrier, inc=1, device_id=(dp, to), device_id_type=MESH)
    pl.semaphore_wait(barrier, 4 + shares - 1 + quarters - 1)

    ups = (odd, 1 - odd)
    sides = [dp_near[-1] + up * (dp_near[1] - dp_near[-1]) for up in ups]

    def halo(s, h):
        land = 1 - ups[s]
        return remote(
            half(h),
            wins[h].at[2 * land],
            halo_send.at[s, h],
            halo_recv.at[land, h],
            sides[s],
            code,
        )

    halos = [halo(s, h) for h in range(halves) for s in range(2)]
    for copy in halos:
        copy.start()

    def norms(w, h):
        wide = wins[h][w].astype(jnp.float32)
        norm = jnp.sum(wide * wide, axis=1, keepdims=True)
        col_b[w, h * LANES : (h + 1) * LANES, :] = jnp.broadcast_to(
            norm * (-LOG2E / SOFTMAX_TEMP), (LANES, LANES)
        )

    for h in range(halves):
        own_copies[h].wait()
        norms(1, h)

    eye = lax.broadcasted_iota(jnp.int32, (LANES, LANES), 0) == lax.broadcasted_iota(
        jnp.int32, (LANES, LANES), 1
    )

    def to_lanes(column):
        return jnp.sum(jnp.where(eye[None], column, 0.0), axis=1)

    def to_column(row):
        square = jnp.where(eye, jnp.broadcast_to(row, (LANES, LANES)), 0.0)
        return jnp.broadcast_to(jnp.sum(square, axis=1, keepdims=True), (LANES, LANES))

    for h in range(halves):
        for s in range(2):
            remote(
                half(h), wins[h].at[2 * s], halo_send.at[s, h], halo_recv.at[s, h], dp, code
            ).wait_recv()

        def score(b, carry):
            if h == 0:
                feat_copy(b).wait()
            inner = lax.dot_general(
                wins[h][places[b]],
                feat[pl.ds(pl.multiple_of(b * block_rows, block_rows), block_rows), :],
                (((1,), (1,)), ((), ())),
                preferred_element_type=jnp.float32,
            )
            scaled = inner.astype(jnp.bfloat16).astype(jnp.float32) * (2.0 * LOG2E / SOFTMAX_TEMP)
            for t in range(block_tiles):
                cells[b * block_tiles + t, h * LANES : (h + 1) * LANES, :] = scaled[
                    :, t * LANES : (t + 1) * LANES
                ]
            return carry

        lax.fori_loop(0, blocks, score, 0)
        norms(0, h)
        norms(2, h)
    for copy in halos:
        copy.wait_send()

    def row_block(r, owner, i):
        b = owner * held + i
        bias = col_b[places[b]]
        for t in range(block_tiles):
            x = (cells[b * block_tiles + t] + bias).reshape(size // SUB, SUB, LANES)
            m8 = jnp.max(x, axis=0)
            s8 = jnp.sum(jnp.exp2(x - m8[None]), axis=0)
            m = jnp.max(m8, axis=0, keepdims=True)
            s = jnp.sum(s8 * jnp.exp2(m8 - m), axis=0, keepdims=True)
            lse_src[r, owner, i, t : t + 1, :] = m + jnp.log2(s)

    def join(parts):
        m = jnp.max(parts, axis=0)
        return m + jnp.log2(jnp.sum(jnp.exp2(parts - m[None]), axis=0))

    def row_update(r):
        for owner in range(shares):
            for b in range(owner * held, (owner + 1) * held):
                row_block(r, owner, b - owner * held)

            @pl.when(share != owner)
            def _():
                remote(
                    lse_src.at[r, owner],
                    lse_in.at[r, share],
                    lse_send.at[r],
                    lse_recv.at[r],
                    dp,
                    owners[owner],
                ).start()

        lse_in[r, share] = lse_src[r, share]
        others = pl.ds(0, shares - 1)
        first = remote(
            lse_src.at[r, others], lse_in.at[r, others], lse_send.at[r], lse_recv.at[r], dp, code
        )
        first.wait_recv()
        value = join(lse_in[r])
        mid_src[r] = value
        for to in far_mates:
            remote(
                mid_src.at[r], mid_in.at[r, quarter], mid_send.at[r], mid_recv.at[r], dp, to
            ).start()
        mid_in[r, quarter] = value
        some = pl.ds(0, quarters - 1)
        second = remote(
            mid_in.at[r, some], mid_in.at[r, some], mid_send.at[r], mid_recv.at[r], dp, code
        )
        second.wait_recv()
        value = -join(mid_in[r])
        row_src[r] = value
        for _, to in mates:
            remote(
                row_src.at[r], row_in.at[r, share], row_send.at[r], row_recv.at[r, share], dp, to
            ).start()
        row_in[r, share] = value

    def row_arrives(r, some):
        for owner in range(some[0] // held, some[-1] // held + 1):

            @pl.when(share != owner)
            def _():
                remote(
                    row_src.at[r],
                    row_in.at[r, owner],
                    row_send.at[r],
                    row_recv.at[r, owner],
                    dp,
                    code,
                ).wait_recv()

            for i in range(held):
                for t in range(block_tiles):
                    row_b[(owner * held + i) * block_tiles + t] = jnp.broadcast_to(
                        row_in[r, owner, i, t : t + 1, :], (SUB, LANES)
                    )

    def row_sent(r):
        others, some = pl.ds(0, shares - 1), pl.ds(0, quarters - 1)
        remote(
            lse_src.at[r, others], lse_in.at[r, others], lse_send.at[r], lse_recv.at[r], dp, code
        ).wait_send()
        remote(
            mid_in.at[r, some], mid_in.at[r, some], mid_send.at[r], mid_recv.at[r], dp, code
        ).wait_send()
        remote(
            row_in.at[r, others], row_in.at[r, others], row_send.at[r], row_recv.at[r, 0], dp, code
        ).wait_send()

    def col_update(r, target):
        def one_tile(j, some):
            span = pl.ds(pl.multiple_of(j * SUB, SUB), SUB)
            tiles_of = pl.ds(some[0] * block_tiles, len(some) * block_tiles)
            x = cells[tiles_of, span, :] + row_b[tiles_of]
            x = x.reshape(len(some), block_tiles, SUB, LANES)
            at = [jnp.full((SUB, LANES), places[b], jnp.int32) for b in some]
            tops = [jnp.max(x[i], axis=0) for i in range(len(some))]
            peaks, olds = [], []
            for w in range(3):
                kept = [jnp.where(at[i] == w, tops[i], LOWEST) for i in range(len(some))]
                if some[0] > 0:
                    olds.append(peak[w, span, :])
                    kept.append(olds[w])
                peaks.append(functools.reduce(jnp.maximum, kept))
            sums = []
            for i in range(len(some)):
                top = jnp.where(at[i] == 0, peaks[0], jnp.where(at[i] == 1, peaks[1], peaks[2]))
                sums.append(jnp.sum(jnp.exp2(x[i] - top[None]), axis=0))
            for w in range(3):
                kept = [jnp.where(at[i] == w, sums[i], 0.0) for i in range(len(some))]
                if some[0] > 0:
                    kept.append(total[w, span, :] * jnp.exp2(olds[w] - peaks[w]))
                peak[w, span, :] = peaks[w]
                total[w, span, :] = functools.reduce(jnp.add, kept)

        def tile_loop(first, last, some):
            def two_tiles(j, carry):
                one_tile(2 * j, some)
                one_tile(2 * j + 1, some)
                return carry

            lax.fori_loop(first // 2, last // 2, two_tiles, 0)

        half_tiles = LANES // SUB
        early, late = range(blocks // 2), range(blocks // 2, blocks)
        row_arrives(r, early)
        tile_loop(0, size // SUB, early)
        row_arrives(r, late)
        mines, copies = [], []
        for h in range(halves):
            tile_loop(h * half_tiles, (h + 1) * half_tiles, late)
            span = slice(h * LANES, (h + 1) * LANES)
            tops, sums = peak[:, span, :], total[:, span, :]
            m = jnp.max(tops, axis=2, keepdims=True)
            s = jnp.sum(sums * jnp.exp2(tops - m), axis=2, keepdims=True)
            mine = to_lanes(jnp.broadcast_to(m, tops.shape)) + jnp.log2(
                to_lanes(jnp.broadcast_to(s, sums.shape))
            )
            mines.append(mine)
            for w in range(3):
                col_src[r, h, w] = mine[w : w + 1]
            for slot, (step, start, count, there) in enumerate(
                ((-2, 0, 1, col_r2), (2, 2, 1, col_l2), (-1, 0, 2, col_r1), (1, 1, 2, col_l1))
            ):
                copies.append(
                    remote(
                        col_src.at[r, h, pl.ds(start, count)],
                        there.at[r, h],
                        col_send.at[r, h, slot],
                        col_recv.at[r, h, slot],
                        dp_near[step],
                        code,
                    )
                )
                copies[-1].start()
        for h in range(halves):
            for copy in copies[4 * h : 4 * h + 4]:
                copy.wait_recv()
            mine, l1, r1 = mines[h], col_l1[r, h], col_r1[r, h]
            sets = (
                (col_l2[r, h, 0], l1[0], mine[0:1]),
                (l1[1], mine[1:2], r1[0]),
                (mine[2:3], r1[1], col_r2[r, h, 0]),
            )
            for w, terms in enumerate(sets):
                m = functools.reduce(jnp.maximum, terms)
                s = functools.reduce(jnp.add, [jnp.exp2(term - m) for term in terms])
                value = target - (m + jnp.log2(s))
                col_b[w, h * LANES : (h + 1) * LANES, :] = to_column(value)
        for copy in copies:
            copy.wait_send()
        row_sent(r)

    target = math.log2((rows * n_dp) / (size * n_dp * n_code))

    def sweep(r, carry):
        row_update(r)
        col_update(r, target)
        return carry

    lax.fori_loop(0, ROUNDS, sweep, 0)
    row_update(ROUNDS)
    pack = 2 * SUB

    def weigh(some):
        def body(j, carry):
            span = pl.ds(pl.multiple_of(j * pack, pack), pack)
            sums = [jnp.zeros((2, SUB, LANES), jnp.float32) for w in range(3)]
            for b in some:
                g = col_b[places[b], span, :].reshape(2, SUB, LANES)
                here = jnp.zeros((2, SUB, LANES), jnp.float32)
                for t in range(block_tiles):
                    d = b * block_tiles + t
                    x = cells[d, span, :].reshape(2, SUB, LANES) + row_b[d][None] + g
                    value = jnp.exp2(x)
                    here = here + value
                    low = value.reshape(pack, LANES).astype(jnp.bfloat16)
                    weight[b, span, t * LANES : (t + 1) * LANES] = low
                at = jnp.full((2, SUB, LANES), places[b], jnp.int32)
                for w in range(3):
                    sums[w] = sums[w] + jnp.where(at == w, here, 0.0)
            for w in range(3):
                part = sums[w].reshape(pack, LANES)
                total[w, span, :] = part if some[0] == 0 else total[w, span, :] + part
            return carry

        lax.fori_loop(0, size // pack, body, 0)

    for some in (range(blocks // 2), range(blocks // 2, blocks)):
        row_arrives(ROUNDS, some)
        weigh(some)
    row_sent(ROUNDS)

    mass = jnp.sum(total[...], axis=2, keepdims=True)
    mass = jnp.broadcast_to(mass, total.shape)
    for h in range(halves):
        part = to_lanes(mass[:, h * LANES : (h + 1) * LANES, :])
        mass_src[:, h, :] = part.astype(jnp.bfloat16).astype(jnp.float32)
    mass_copies = [
        remote(
            mass_src.at[pl.ds(2 * s, 1)],
            mass_in.at[1 - s],
            mass_send.at[s],
            mass_recv.at[1 - s],
            dp_near[2 * s - 1],
            code,
        )
        for s in range(2)
    ]
    for copy in mass_copies:
        copy.start()

    def columns(n):
        return pl.ds(pl.multiple_of(n * piece, piece), piece)

    def num_copy(s, n):
        land = 1 - ups[s]
        return remote(
            num_src.at[s, n],
            num_in.at[land, n],
            num_send.at[s, n],
            num_recv.at[land, n],
            sides[s],
            code,
        )

    def numerators(n, carry):
        for w in range(3):
            num_sum[n, w] = jnp.zeros((size, piece), jnp.float32)

        def two_blocks(step, carry):
            products = []
            for b in (2 * step, 2 * step + 1):
                span = pl.ds(pl.multiple_of(b * block_rows, block_rows), block_rows)
                product = jnp.dot(
                    weight[b], feat[span, columns(n)], preferred_element_type=jnp.float32
                )
                products.append((jnp.full(product.shape, places[b], jnp.int32), product))
            for w in range(3):
                kept = [jnp.where(at == w, product, 0.0) for at, product in products]
                num_sum[n, w] = num_sum[n, w] + (kept[0] + kept[1])
            return carry

        lax.fori_loop(0, blocks // 2, two_blocks, 0)
        for s in range(2):
            num_src[s, n] = num_sum[n, 2 * ups[s]].astype(jnp.bfloat16)
            num_copy(s, n).start()
        return carry

    lax.fori_loop(0, PIECES, numerators, 0)

    for s in range(2):
        remote(
            mass_src.at[pl.ds(0, 1)], mass_in.at[s], mass_send.at[s], mass_recv.at[s], dp, code
        ).wait_recv()
    for copy in mass_copies:
        copy.wait_send()
    mass_all = mass_in[0, 0] + mass_src[1] + mass_in[1, 0]
    mass_ref[...] = mass_all
    for h in range(halves):
        peak[0, h * LANES : (h + 1) * LANES, :] = to_column(mass_all[h : h + 1])

    def finish(n, carry):
        for s in range(2):
            remote(
                num_src.at[s, n], num_in.at[s, n], num_send.at[s, n], num_recv.at[s, n], dp, code
            ).wait()
        own = num_sum[n, 1].astype(jnp.bfloat16).astype(jnp.float32)
        whole = num_in[0, n].astype(jnp.float32) + own + num_in[1, n].astype(jnp.float32)
        divisor = jnp.concatenate([peak[0]] * (piece // LANES), axis=1)
        out_ref[:, columns(n)] = (whole / divisor).astype(jnp.bfloat16)
        return carry

    lax.fori_loop(0, PIECES, finish, 0)


def pass_on(new_ref, mass_in_ref, out_ref, mass_ref, sems):
    copies = [
        pltpu.make_async_copy(new_ref, out_ref, sems.at[0]),
        pltpu.make_async_copy(mass_in_ref, mass_ref, sems.at[1]),
    ]
    for copy in copies:
        copy.start()
    for copy in copies:
        copy.wait()


def solution(mesh):
    n_dp, n_code = mesh.shape["dp"], mesh.shape["code"]

    def local(features, centroids, block_lists):
        rows, width = features.shape
        size = centroids.shape[0]
        tiles = rows // LANES
        blocks = block_lists.shape[0]
        block_tiles = tiles // blocks
        shares = NEAR * (n_code // Z)
        mine = (blocks // shares, block_tiles, LANES)
        halves = size // LANES
        piece = width // PIECES
        updates = ROUNDS + 1
        f32, bf16 = jnp.float32, jnp.bfloat16
        dma = pltpu.SemaphoreType.DMA
        new_centroids, mass = pl.pallas_call(
            functools.partial(kernel, n_dp, n_code),
            out_shape=(
                jax.ShapeDtypeStruct((size, width), bf16),
                jax.ShapeDtypeStruct((halves, LANES), f32),
            ),
            in_specs=[
                pl.BlockSpec(memory_space=pltpu.SMEM),
                pl.BlockSpec(memory_space=pl.ANY),
                pl.BlockSpec(memory_space=pl.ANY),
            ],
            out_specs=(
                pl.BlockSpec(memory_space=pltpu.VMEM),
                pl.BlockSpec(memory_space=pltpu.VMEM),
            ),
            scratch_shapes=[
                pltpu.VMEM((rows, width), bf16),
                pltpu.VMEM((3, size // halves, width), bf16),
                pltpu.VMEM((3, size // halves, width), bf16),
                pltpu.VMEM((tiles, size, LANES), f32),
                pltpu.VMEM((tiles, SUB, LANES), f32),
                pltpu.VMEM((3, size, LANES), f32),
                pltpu.VMEM((3, size, LANES), f32),
                pltpu.VMEM((3, size, LANES), f32),
                pltpu.VMEM((blocks, size, rows // blocks), bf16),
                pltpu.SMEM((blocks,), jnp.int32),
                pltpu.VMEM((updates, shares, *mine), f32),
                pltpu.VMEM((updates, shares, *mine), f32),
                pltpu.VMEM((updates, *mine), f32),
                pltpu.VMEM((updates, Z // NEAR, *mine), f32),
                pltpu.VMEM((updates, *mine), f32),
                pltpu.VMEM((updates, shares, *mine), f32),
                pltpu.VMEM((ROUNDS, halves, 3, 1, LANES), f32),
                pltpu.VMEM((ROUNDS, halves, 1, 1, LANES), f32),
                pltpu.VMEM((ROUNDS, halves, 2, 1, LANES), f32),
                pltpu.VMEM((ROUNDS, halves, 2, 1, LANES), f32),
                pltpu.VMEM((ROUNDS, halves, 1, 1, LANES), f32),
                pltpu.VMEM((3, halves, LANES), f32),
                pltpu.VMEM((2, 1, halves, LANES), f32),
                pltpu.VMEM((2, PIECES, size, piece), bf16),
                pltpu.VMEM((2, PIECES, size, piece), bf16),
                pltpu.VMEM((PIECES, 3, size, piece), f32),
                dma((blocks,)),
                dma((halves,)),
                dma((2, halves)),
                dma((2, halves)),
                dma((updates,)),
                dma((updates,)),
                dma((updates,)),
                dma((updates,)),
                dma((updates,)),
                dma((updates, shares)),
                dma((ROUNDS, halves, 4)),
                dma((ROUNDS, halves, 4)),
                dma((2,)),
                dma((2,)),
                dma((2, PIECES)),
                dma((2, PIECES)),
            ],
            compiler_params=pltpu.CompilerParams(
                collective_id=0, has_side_effects=True, vmem_limit_bytes=56 * 1024 * 1024
            ),
            cost_estimate=pl.CostEstimate(
                flops=8 * rows * size * width,
                bytes_accessed=2 * (rows + 2 * size) * width,
                transcendentals=8 * rows * size,
            ),
            name="balanced_kmeans",
        )(block_lists, features, centroids)
        new_centroids, mass = pl.pallas_call(
            pass_on,
            out_shape=(
                jax.ShapeDtypeStruct((size, width), bf16),
                jax.ShapeDtypeStruct((halves, LANES), f32),
            ),
            in_specs=[pl.BlockSpec(memory_space=pl.ANY)] * 2,
            out_specs=(pl.BlockSpec(memory_space=pl.ANY),) * 2,
            scratch_shapes=[dma((2,))],
            cost_estimate=pl.CostEstimate(
                flops=0, bytes_accessed=4 * size * width, transcendentals=0
            ),
            name="pass_on",
        )(new_centroids, mass)
        return new_centroids, mass.reshape(size)

    return jax.shard_map(
        local,
        mesh=mesh,
        in_specs=(P("dp", None), P(("code", "dp"), None), P("dp", None)),
        out_specs=(P(("code", "dp"), None), P(("code", "dp"))),
        check_vma=False,
    )
```

```python
import functools
import math

import jax
import jax.numpy as jnp
from jax import lax
from jax.experimental import pallas as pl
from jax.experimental.pallas import tpu as pltpu
from jax.sharding import PartitionSpec as P

ROUNDS = 3
SOFTMAX_TEMP = 12.0
LOG2E = math.log2(math.e)
LOWEST = -3.0e38
LANES = 128
SUB = 8
PIECES = 3
Z = 16
NEAR = 2
MESH = pl.DeviceIdType.MESH


def kernel(
    n_dp,
    n_code,
    lists_ref,
    feat_hbm,
    cent_hbm,
    whole_ref,
    mass_ref,
    feat,
    win,
    cells,
    row_b,
    col_b,
    peak,
    total,
    weight,
    places,
    lse_src,
    lse_in,
    mid_src,
    mid_in,
    row_src,
    row_in,
    col_src,
    col_l2,
    col_l1,
    col_r1,
    col_r2,
    mass_src,
    mass_in,
    num_src,
    num_in,
    num_sum,
    feat_sem,
    own_sem,
    halo_send,
    halo_recv,
    lse_send,
    lse_recv,
    mid_send,
    mid_recv,
    row_send,
    row_recv,
    col_send,
    col_recv,
    mass_send,
    mass_recv,
    num_send,
    num_recv,
):
    dp = lax.axis_index("dp")
    code = lax.axis_index("code")
    blocks = lists_ref.shape[0]
    rows = feat.shape[0]
    block_rows = rows // blocks
    block_tiles = block_rows // LANES
    tiles = rows // LANES
    size, width = win.shape[1], win.shape[2]
    halves = size // LANES
    piece = width // PIECES
    odd = lax.rem(dp, 2)
    dp_near = {step: lax.rem(dp + (n_dp + step), n_dp) for step in (-2, -1, 1, 2)}
    for b in range(blocks):
        places[b] = jnp.minimum(lax.rem(lists_ref[b, code] + (n_dp + 1) - dp, n_dp), 2)

    y_hi, z = lax.div(code, Z), lax.rem(code, Z)
    quarter, near = lax.div(z, NEAR), lax.rem(z, NEAR)
    quarters, shares = Z // NEAR, NEAR * (n_code // Z)
    share = y_hi * NEAR + near
    held = blocks // shares
    mates = []
    for step in range(1, shares):
        other = lax.rem(share + step, shares)
        at = lax.div(other, NEAR) * Z + quarter * NEAR + lax.rem(other, NEAR)
        mates.append((other, at))
    owners = [(b // NEAR) * Z + quarter * NEAR + b % NEAR for b in range(shares)]
    far_mates = []
    for step in sorted(range(1, quarters), key=lambda step: abs(2 * step - quarters)):
        far_mates.append(y_hi * Z + lax.rem(quarter + step, quarters) * NEAR + near)

    def feat_copy(b):
        span = pl.ds(b * block_rows, block_rows)
        return pltpu.make_async_copy(feat_hbm.at[span], feat.at[span], feat_sem.at[b])

    def remote(src, dst, send, recv, to_dp, to_code):
        return pltpu.make_async_remote_copy(
            src_ref=src,
            dst_ref=dst,
            send_sem=send,
            recv_sem=recv,
            device_id=(to_dp, to_code),
            device_id_type=MESH,
        )

    own_copy = pltpu.make_async_copy(cent_hbm, win.at[1], own_sem)
    own_copy.start()
    for b in range(blocks):
        feat_copy(b).start()

    barrier = pltpu.get_barrier_semaphore()
    for step in (-1, 1, -2, 2):
        pl.semaphore_signal(
            barrier, inc=1, device_id=(dp_near[step], code), device_id_type=MESH
        )
    for to in [at for _, at in mates] + far_mates:
        pl.semaphore_signal(barrier, inc=1, device_id=(dp, to), device_id_type=MESH)
    pl.semaphore_wait(barrier, 4 + shares - 1 + quarters - 1)

    ups = (odd, 1 - odd)
    sides = [dp_near[-1] + up * (dp_near[1] - dp_near[-1]) for up in ups]

    def halo(s):
        land = 1 - ups[s]
        return remote(
            cent_hbm, win.at[2 * land], halo_send.at[s], halo_recv.at[land], sides[s], code
        )

    halo(0).start()
    halo(1).start()

    def norms(w):
        wide = win[w].astype(jnp.float32)
        norm = jnp.sum(wide * wide, axis=1, keepdims=True)
        col_b[w] = jnp.broadcast_to(norm * (-LOG2E / SOFTMAX_TEMP), (size, LANES))

    own_copy.wait()
    norms(1)
    for s in range(2):
        halo(s).wait_send()
    for s in range(2):
        remote(cent_hbm, win.at[2 * s], halo_send.at[s], halo_recv.at[s], dp, code).wait_recv()

    eye = lax.broadcasted_iota(jnp.int32, (LANES, LANES), 0) == lax.broadcasted_iota(
        jnp.int32, (LANES, LANES), 1
    )

    def to_lanes(column):
        return jnp.sum(jnp.where(eye[None], column, 0.0), axis=1)

    def to_column(row):
        square = jnp.where(eye, jnp.broadcast_to(row, (LANES, LANES)), 0.0)
        return jnp.broadcast_to(jnp.sum(square, axis=1, keepdims=True), (LANES, LANES))

    def score(b):
        inner = lax.dot_general(
            win[places[b]],
            feat[pl.ds(pl.multiple_of(b * block_rows, block_rows), block_rows), :],
            (((1,), (1,)), ((), ())),
            preferred_element_type=jnp.float32,
        )
        scaled = inner.astype(jnp.bfloat16).astype(jnp.float32) * (2.0 * LOG2E / SOFTMAX_TEMP)
        for t in range(block_tiles):
            cells[b * block_tiles + t] = scaled[:, t * LANES : (t + 1) * LANES]

    def two_scores(step, carry):
        feat_copy(2 * step).wait()
        feat_copy(2 * step + 1).wait()
        score(2 * step)
        score(2 * step + 1)
        return carry

    lax.fori_loop(0, blocks // 2, two_scores, 0)
    norms(0)
    norms(2)

    def row_block(r, owner, i):
        b = owner * held + i
        bias = col_b[places[b]]
        for t in range(block_tiles):
            x = (cells[b * block_tiles + t] + bias).reshape(size // SUB, SUB, LANES)
            m8 = jnp.max(x, axis=0)
            s8 = jnp.sum(jnp.exp2(x - m8[None]), axis=0)
            m = jnp.max(m8, axis=0, keepdims=True)
            s = jnp.sum(s8 * jnp.exp2(m8 - m), axis=0, keepdims=True)
            lse_src[r, owner, i, t : t + 1, :] = m + jnp.log2(s)

    def join(parts):
        m = jnp.max(parts, axis=0)
        return m + jnp.log2(jnp.sum(jnp.exp2(parts - m[None]), axis=0))

    def row_update(r):
        for owner in range(shares):
            for b in range(owner * held, (owner + 1) * held):
                row_block(r, owner, b - owner * held)

            @pl.when(share != owner)
            def _():
                remote(
                    lse_src.at[r, owner],
                    lse_in.at[r, share],
                    lse_send.at[r],
                    lse_recv.at[r],
                    dp,
                    owners[owner],
                ).start()

        lse_in[r, share] = lse_src[r, share]
        others = pl.ds(0, shares - 1)
        first = remote(
            lse_src.at[r, others], lse_in.at[r, others], lse_send.at[r], lse_recv.at[r], dp, code
        )
        first.wait_recv()
        value = join(lse_in[r])
        mid_src[r] = value
        for to in far_mates:
            remote(
                mid_src.at[r], mid_in.at[r, quarter], mid_send.at[r], mid_recv.at[r], dp, to
            ).start()
        mid_in[r, quarter] = value
        some = pl.ds(0, quarters - 1)
        second = remote(
            mid_in.at[r, some], mid_in.at[r, some], mid_send.at[r], mid_recv.at[r], dp, code
        )
        second.wait_recv()
        value = -join(mid_in[r])
        row_src[r] = value
        for _, to in mates:
            remote(
                row_src.at[r], row_in.at[r, share], row_send.at[r], row_recv.at[r, share], dp, to
            ).start()
        row_in[r, share] = value

    def row_arrives(r, some):
        for owner in range(some[0] // held, some[-1] // held + 1):

            @pl.when(share != owner)
            def _():
                remote(
                    row_src.at[r],
                    row_in.at[r, owner],
                    row_send.at[r],
                    row_recv.at[r, owner],
                    dp,
                    code,
                ).wait_recv()

            for i in range(held):
                for t in range(block_tiles):
                    row_b[(owner * held + i) * block_tiles + t] = jnp.broadcast_to(
                        row_in[r, owner, i, t : t + 1, :], (SUB, LANES)
                    )

    def row_sent(r):
        others, some = pl.ds(0, shares - 1), pl.ds(0, quarters - 1)
        remote(
            lse_src.at[r, others], lse_in.at[r, others], lse_send.at[r], lse_recv.at[r], dp, code
        ).wait_send()
        remote(
            mid_in.at[r, some], mid_in.at[r, some], mid_send.at[r], mid_recv.at[r], dp, code
        ).wait_send()
        remote(
            row_in.at[r, others], row_in.at[r, others], row_send.at[r], row_recv.at[r, 0], dp, code
        ).wait_send()

    def col_update(r, target):
        def one_tile(j, some):
            span = pl.ds(pl.multiple_of(j * SUB, SUB), SUB)
            tiles_of = pl.ds(some[0] * block_tiles, len(some) * block_tiles)
            x = cells[tiles_of, span, :] + row_b[tiles_of]
            x = x.reshape(len(some), block_tiles, SUB, LANES)
            at = [jnp.full((SUB, LANES), places[b], jnp.int32) for b in some]
            tops = [jnp.max(x[i], axis=0) for i in range(len(some))]
            peaks, olds = [], []
            for w in range(3):
                kept = [jnp.where(at[i] == w, tops[i], LOWEST) for i in range(len(some))]
                if some[0] > 0:
                    olds.append(peak[w, span, :])
                    kept.append(olds[w])
                peaks.append(functools.reduce(jnp.maximum, kept))
            sums = []
            for i in range(len(some)):
                top = jnp.where(at[i] == 0, peaks[0], jnp.where(at[i] == 1, peaks[1], peaks[2]))
                sums.append(jnp.sum(jnp.exp2(x[i] - top[None]), axis=0))
            for w in range(3):
                kept = [jnp.where(at[i] == w, sums[i], 0.0) for i in range(len(some))]
                if some[0] > 0:
                    kept.append(total[w, span, :] * jnp.exp2(olds[w] - peaks[w]))
                peak[w, span, :] = peaks[w]
                total[w, span, :] = functools.reduce(jnp.add, kept)

        def tile_loop(first, last, some):
            def two_tiles(j, carry):
                one_tile(2 * j, some)
                one_tile(2 * j + 1, some)
                return carry

            lax.fori_loop(first // 2, last // 2, two_tiles, 0)

        half_tiles = LANES // SUB
        early, late = range(blocks // 2), range(blocks // 2, blocks)
        row_arrives(r, early)
        tile_loop(0, size // SUB, early)
        row_arrives(r, late)
        mines, copies = [], []
        for h in range(halves):
            tile_loop(h * half_tiles, (h + 1) * half_tiles, late)
            span = slice(h * LANES, (h + 1) * LANES)
            tops, sums = peak[:, span, :], total[:, span, :]
            m = jnp.max(tops, axis=2, keepdims=True)
            s = jnp.sum(sums * jnp.exp2(tops - m), axis=2, keepdims=True)
            mine = to_lanes(jnp.broadcast_to(m, tops.shape)) + jnp.log2(
                to_lanes(jnp.broadcast_to(s, sums.shape))
            )
            mines.append(mine)
            for w in range(3):
                col_src[r, h, w] = mine[w : w + 1]
            for slot, (step, start, count, there) in enumerate(
                ((-2, 0, 1, col_r2), (2, 2, 1, col_l2), (-1, 0, 2, col_r1), (1, 1, 2, col_l1))
            ):
                copies.append(
                    remote(
                        col_src.at[r, h, pl.ds(start, count)],
                        there.at[r, h],
                        col_send.at[r, h, slot],
                        col_recv.at[r, h, slot],
                        dp_near[step],
                        code,
                    )
                )
                copies[-1].start()
        for h in range(halves):
            for copy in copies[4 * h : 4 * h + 4]:
                copy.wait_recv()
            mine, l1, r1 = mines[h], col_l1[r, h], col_r1[r, h]
            sets = (
                (col_l2[r, h, 0], l1[0], mine[0:1]),
                (l1[1], mine[1:2], r1[0]),
                (mine[2:3], r1[1], col_r2[r, h, 0]),
            )
            for w, terms in enumerate(sets):
                m = functools.reduce(jnp.maximum, terms)
                s = functools.reduce(jnp.add, [jnp.exp2(term - m) for term in terms])
                value = target - (m + jnp.log2(s))
                col_b[w, h * LANES : (h + 1) * LANES, :] = to_column(value)
        for copy in copies:
            copy.wait_send()
        row_sent(r)

    target = math.log2((rows * n_dp) / (size * n_dp * n_code))

    def sweep(r, carry):
        row_update(r)
        col_update(r, target)
        return carry

    lax.fori_loop(0, ROUNDS, sweep, 0)
    row_update(ROUNDS)
    pack = 2 * SUB

    def weigh(some):
        def body(j, carry):
            span = pl.ds(pl.multiple_of(j * pack, pack), pack)
            sums = [jnp.zeros((2, SUB, LANES), jnp.float32) for w in range(3)]
            for b in some:
                g = col_b[places[b], span, :].reshape(2, SUB, LANES)
                here = jnp.zeros((2, SUB, LANES), jnp.float32)
                for t in range(block_tiles):
                    d = b * block_tiles + t
                    x = cells[d, span, :].reshape(2, SUB, LANES) + row_b[d][None] + g
                    value = jnp.exp2(x)
                    here = here + value
                    low = value.reshape(pack, LANES).astype(jnp.bfloat16)
                    weight[b, span, t * LANES : (t + 1) * LANES] = low
                at = jnp.full((2, SUB, LANES), places[b], jnp.int32)
                for w in range(3):
                    sums[w] = sums[w] + jnp.where(at == w, here, 0.0)
            for w in range(3):
                part = sums[w].reshape(pack, LANES)
                total[w, span, :] = part if some[0] == 0 else total[w, span, :] + part
            return carry

        lax.fori_loop(0, size // pack, body, 0)

    for some in (range(blocks // 2), range(blocks // 2, blocks)):
        row_arrives(ROUNDS, some)
        weigh(some)
    row_sent(ROUNDS)

    mass = jnp.sum(total[...], axis=2, keepdims=True)
    mass = jnp.broadcast_to(mass, total.shape)
    for h in range(halves):
        part = to_lanes(mass[:, h * LANES : (h + 1) * LANES, :])
        mass_src[:, h, :] = part.astype(jnp.bfloat16).astype(jnp.float32)
    mass_copies = [
        remote(
            mass_src.at[pl.ds(2 * s, 1)],
            mass_in.at[1 - s],
            mass_send.at[s],
            mass_recv.at[1 - s],
            dp_near[2 * s - 1],
            code,
        )
        for s in range(2)
    ]
    for copy in mass_copies:
        copy.start()

    def columns(n):
        return pl.ds(pl.multiple_of(n * piece, piece), piece)

    def num_copy(s, n):
        land = 1 - ups[s]
        return remote(
            num_src.at[s, n],
            num_in.at[land, n],
            num_send.at[s, n],
            num_recv.at[land, n],
            sides[s],
            code,
        )

    def numerators(n, carry):
        products = []
        for b in range(blocks):
            product = jnp.dot(
                weight[b],
                feat[b * block_rows : (b + 1) * block_rows, columns(n)],
                preferred_element_type=jnp.float32,
            )
            products.append((jnp.full(product.shape, places[b], jnp.int32), product))
        for w in range(3):
            kept = [jnp.where(at == w, product, 0.0) for at, product in products]
            num_sum[n, w] = functools.reduce(jnp.add, kept)
        for s in range(2):
            num_src[s, n] = num_sum[n, 2 * ups[s]].astype(jnp.bfloat16)
            num_copy(s, n).start()
        return carry

    lax.fori_loop(0, PIECES, numerators, 0)

    for s in range(2):
        remote(
            mass_src.at[pl.ds(0, 1)], mass_in.at[s], mass_send.at[s], mass_recv.at[s], dp, code
        ).wait_recv()
    for copy in mass_copies:
        copy.wait_send()
    mass_ref[...] = mass_in[0, 0] + mass_src[1] + mass_in[1, 0]

    def finish(n, carry):
        for s in range(2):
            remote(
                num_src.at[s, n], num_in.at[s, n], num_send.at[s, n], num_recv.at[s, n], dp, code
            ).wait()
        own = num_sum[n, 1].astype(jnp.bfloat16).astype(jnp.float32)
        whole_ref[n] = (
            num_in[0, n].astype(jnp.float32) + own + num_in[1, n].astype(jnp.float32)
        )
        return carry

    lax.fori_loop(0, PIECES, finish, 0)


def divide(whole_ref, mass_in_ref, out_ref, mass_ref):
    size, piece = whole_ref.shape[1], whole_ref.shape[2]
    eye = lax.broadcasted_iota(jnp.int32, (LANES, LANES), 0) == lax.broadcasted_iota(
        jnp.int32, (LANES, LANES), 1
    )
    mass_ref[...] = mass_in_ref[...]
    for h in range(size // LANES):
        row = jnp.broadcast_to(mass_in_ref[h : h + 1, :], (LANES, LANES))
        column = jnp.sum(jnp.where(eye, row, 0.0), axis=1, keepdims=True)
        span = slice(h * LANES, (h + 1) * LANES)
        for n in range(PIECES):
            value = whole_ref[n, span, :] / column
            out_ref[span, n * piece : (n + 1) * piece] = value.astype(out_ref.dtype)


def solution(mesh):
    n_dp, n_code = mesh.shape["dp"], mesh.shape["code"]

    def local(features, centroids, block_lists):
        rows, width = features.shape
        size = centroids.shape[0]
        tiles = rows // LANES
        blocks = block_lists.shape[0]
        block_tiles = tiles // blocks
        shares = NEAR * (n_code // Z)
        mine = (blocks // shares, block_tiles, LANES)
        halves = size // LANES
        piece = width // PIECES
        updates = ROUNDS + 1
        f32, bf16 = jnp.float32, jnp.bfloat16
        dma = pltpu.SemaphoreType.DMA
        whole, mass = pl.pallas_call(
            functools.partial(kernel, n_dp, n_code),
            out_shape=(
                jax.ShapeDtypeStruct((PIECES, size, piece), f32),
                jax.ShapeDtypeStruct((halves, LANES), f32),
            ),
            in_specs=[
                pl.BlockSpec(memory_space=pltpu.SMEM),
                pl.BlockSpec(memory_space=pl.ANY),
                pl.BlockSpec(memory_space=pl.ANY),
            ],
            out_specs=(
                pl.BlockSpec(memory_space=pltpu.VMEM),
                pl.BlockSpec(memory_space=pltpu.VMEM),
            ),
            scratch_shapes=[
                pltpu.VMEM((rows, width), bf16),
                pltpu.VMEM((3, size, width), bf16),
                pltpu.VMEM((tiles, size, LANES), f32),
                pltpu.VMEM((tiles, SUB, LANES), f32),
                pltpu.VMEM((3, size, LANES), f32),
                pltpu.VMEM((3, size, LANES), f32),
                pltpu.VMEM((3, size, LANES), f32),
                pltpu.VMEM((blocks, size, rows // blocks), bf16),
                pltpu.SMEM((blocks,), jnp.int32),
                pltpu.VMEM((updates, shares, *mine), f32),
                pltpu.VMEM((updates, shares, *mine), f32),
                pltpu.VMEM((updates, *mine), f32),
                pltpu.VMEM((updates, Z // NEAR, *mine), f32),
                pltpu.VMEM((updates, *mine), f32),
                pltpu.VMEM((updates, shares, *mine), f32),
                pltpu.VMEM((ROUNDS, halves, 3, 1, LANES), f32),
                pltpu.VMEM((ROUNDS, halves, 1, 1, LANES), f32),
                pltpu.VMEM((ROUNDS, halves, 2, 1, LANES), f32),
                pltpu.VMEM((ROUNDS, halves, 2, 1, LANES), f32),
                pltpu.VMEM((ROUNDS, halves, 1, 1, LANES), f32),
                pltpu.VMEM((3, halves, LANES), f32),
                pltpu.VMEM((2, 1, halves, LANES), f32),
                pltpu.VMEM((2, PIECES, size, piece), bf16),
                pltpu.VMEM((2, PIECES, size, piece), bf16),
                pltpu.VMEM((PIECES, 3, size, piece), f32),
                dma((blocks,)),
                dma,
                dma((2,)),
                dma((2,)),
                dma((updates,)),
                dma((updates,)),
                dma((updates,)),
                dma((updates,)),
                dma((updates,)),
                dma((updates, shares)),
                dma((ROUNDS, halves, 4)),
                dma((ROUNDS, halves, 4)),
                dma((2,)),
                dma((2,)),
                dma((2, PIECES)),
                dma((2, PIECES)),
            ],
            compiler_params=pltpu.CompilerParams(
                collective_id=0, has_side_effects=True, vmem_limit_bytes=56 * 1024 * 1024
            ),
            cost_estimate=pl.CostEstimate(
                flops=8 * rows * size * width,
                bytes_accessed=2 * (rows + 2 * size) * width,
                transcendentals=8 * rows * size,
            ),
            name="balanced_kmeans",
        )(block_lists, features, centroids)
        new_centroids, mass = pl.pallas_call(
            divide,
            out_shape=(
                jax.ShapeDtypeStruct((size, width), bf16),
                jax.ShapeDtypeStruct((halves, LANES), f32),
            ),
            cost_estimate=pl.CostEstimate(
                flops=size * width, bytes_accessed=6 * size * width, transcendentals=0
            ),
            name="divide",
        )(whole, mass)
        return new_centroids, mass.reshape(size)

    return jax.shard_map(
        local,
        mesh=mesh,
        in_specs=(P("dp", None), P(("code", "dp"), None), P("dp", None)),
        out_specs=(P(("code", "dp"), None), P(("code", "dp"))),
        check_vma=False,
    )
```

```python
import functools
import math

import jax
import jax.numpy as jnp
from jax import lax
from jax.experimental import pallas as pl
from jax.experimental.pallas import tpu as pltpu
from jax.sharding import PartitionSpec as P

ROUNDS = 3
SOFTMAX_TEMP = 12.0
LOG2E = math.log2(math.e)
LOWEST = -3.0e38
LANES = 128
SUB = 8
PIECES = 3
Z = 16
NEAR = 2
MESH = pl.DeviceIdType.MESH


def kernel(
    n_dp,
    n_code,
    lists_ref,
    feat_hbm,
    cent_hbm,
    whole_ref,
    mass_ref,
    feat,
    win,
    cells,
    row_b,
    col_b,
    peak,
    total,
    weight,
    places,
    lse_src,
    lse_in,
    mid_src,
    mid_in,
    row_src,
    row_in,
    col_src,
    col_l2,
    col_l1,
    col_r1,
    col_r2,
    mass_src,
    mass_in,
    num_src,
    num_in,
    num_own,
    feat_sem,
    own_sem,
    halo_send,
    halo_recv,
    lse_send,
    lse_recv,
    mid_send,
    mid_recv,
    row_send,
    row_recv,
    col_send,
    col_recv,
    mass_send,
    mass_recv,
    num_send,
    num_recv,
):
    dp = lax.axis_index("dp")
    code = lax.axis_index("code")
    blocks = lists_ref.shape[0]
    rows = feat.shape[0]
    block_rows = rows // blocks
    block_tiles = block_rows // LANES
    tiles = rows // LANES
    size, width = win.shape[1], win.shape[2]
    halves = size // LANES
    piece = width // PIECES
    odd = lax.rem(dp, 2)
    dp_near = {step: lax.rem(dp + (n_dp + step), n_dp) for step in (-2, -1, 1, 2)}
    for b in range(blocks):
        places[b] = jnp.minimum(lax.rem(lists_ref[b, code] + (n_dp + 1) - dp, n_dp), 2)

    y_hi, z = lax.div(code, Z), lax.rem(code, Z)
    quarter, near = lax.div(z, NEAR), lax.rem(z, NEAR)
    quarters, shares = Z // NEAR, NEAR * (n_code // Z)
    share = y_hi * NEAR + near
    held = blocks // shares
    mates = []
    for step in range(1, shares):
        other = lax.rem(share + step, shares)
        at = lax.div(other, NEAR) * Z + quarter * NEAR + lax.rem(other, NEAR)
        mates.append((other, at))
    owners = [(b // NEAR) * Z + quarter * NEAR + b % NEAR for b in range(shares)]
    far_mates = []
    for step in sorted(range(1, quarters), key=lambda step: abs(2 * step - quarters)):
        far_mates.append(y_hi * Z + lax.rem(quarter + step, quarters) * NEAR + near)

    def feat_copy(b):
        span = pl.ds(b * block_rows, block_rows)
        return pltpu.make_async_copy(feat_hbm.at[span], feat.at[span], feat_sem.at[b])

    def remote(src, dst, send, recv, to_dp, to_code):
        return pltpu.make_async_remote_copy(
            src_ref=src,
            dst_ref=dst,
            send_sem=send,
            recv_sem=recv,
            device_id=(to_dp, to_code),
            device_id_type=MESH,
        )

    own_copy = pltpu.make_async_copy(cent_hbm, win.at[1], own_sem)
    own_copy.start()
    for b in range(blocks):
        feat_copy(b).start()

    barrier = pltpu.get_barrier_semaphore()
    for step in (-1, 1, -2, 2):
        pl.semaphore_signal(
            barrier, inc=1, device_id=(dp_near[step], code), device_id_type=MESH
        )
    for to in [at for _, at in mates] + far_mates:
        pl.semaphore_signal(barrier, inc=1, device_id=(dp, to), device_id_type=MESH)
    pl.semaphore_wait(barrier, 4 + shares - 1 + quarters - 1)

    ups = (odd, 1 - odd)
    sides = [dp_near[-1] + up * (dp_near[1] - dp_near[-1]) for up in ups]

    def halo(s):
        land = 1 - ups[s]
        return remote(
            cent_hbm, win.at[2 * land], halo_send.at[s], halo_recv.at[land], sides[s], code
        )

    halo(0).start()
    halo(1).start()

    def norms(w):
        wide = win[w].astype(jnp.float32)
        norm = jnp.sum(wide * wide, axis=1, keepdims=True)
        col_b[w] = jnp.broadcast_to(norm * (-LOG2E / SOFTMAX_TEMP), (size, LANES))

    own_copy.wait()
    norms(1)
    for s in range(2):
        halo(s).wait_send()
    for s in range(2):
        remote(cent_hbm, win.at[2 * s], halo_send.at[s], halo_recv.at[s], dp, code).wait_recv()

    eye = lax.broadcasted_iota(jnp.int32, (LANES, LANES), 0) == lax.broadcasted_iota(
        jnp.int32, (LANES, LANES), 1
    )

    def to_lanes(column):
        return jnp.sum(jnp.where(eye[None], column, 0.0), axis=1)

    def to_column(row):
        square = jnp.where(eye, jnp.broadcast_to(row, (LANES, LANES)), 0.0)
        return jnp.broadcast_to(jnp.sum(square, axis=1, keepdims=True), (LANES, LANES))

    def score(b):
        inner = lax.dot_general(
            win[places[b]],
            feat[pl.ds(pl.multiple_of(b * block_rows, block_rows), block_rows), :],
            (((1,), (1,)), ((), ())),
            preferred_element_type=jnp.float32,
        )
        scaled = inner.astype(jnp.bfloat16).astype(jnp.float32) * (2.0 * LOG2E / SOFTMAX_TEMP)
        for t in range(block_tiles):
            cells[b * block_tiles + t] = scaled[:, t * LANES : (t + 1) * LANES]

    def two_scores(step, carry):
        feat_copy(2 * step).wait()
        feat_copy(2 * step + 1).wait()
        score(2 * step)
        score(2 * step + 1)
        return carry

    lax.fori_loop(0, blocks // 2, two_scores, 0)
    norms(0)
    norms(2)

    def row_block(r, owner, i):
        b = owner * held + i
        bias = col_b[places[b]]
        for t in range(block_tiles):
            x = (cells[b * block_tiles + t] + bias).reshape(size // SUB, SUB, LANES)
            m8 = jnp.max(x, axis=0)
            s8 = jnp.sum(jnp.exp2(x - m8[None]), axis=0)
            m = jnp.max(m8, axis=0, keepdims=True)
            s = jnp.sum(s8 * jnp.exp2(m8 - m), axis=0, keepdims=True)
            lse_src[r, owner, i, t : t + 1, :] = m + jnp.log2(s)

    def join(parts):
        m = jnp.max(parts, axis=0)
        return m + jnp.log2(jnp.sum(jnp.exp2(parts - m[None]), axis=0))

    def row_update(r):
        for owner in range(shares):
            for b in range(owner * held, (owner + 1) * held):
                row_block(r, owner, b - owner * held)

            @pl.when(share != owner)
            def _():
                remote(
                    lse_src.at[r, owner],
                    lse_in.at[r, share],
                    lse_send.at[r],
                    lse_recv.at[r],
                    dp,
                    owners[owner],
                ).start()

        lse_in[r, share] = lse_src[r, share]
        others = pl.ds(0, shares - 1)
        first = remote(
            lse_src.at[r, others], lse_in.at[r, others], lse_send.at[r], lse_recv.at[r], dp, code
        )
        first.wait_recv()
        value = join(lse_in[r])
        mid_src[r] = value
        for to in far_mates:
            remote(
                mid_src.at[r], mid_in.at[r, quarter], mid_send.at[r], mid_recv.at[r], dp, to
            ).start()
        mid_in[r, quarter] = value
        some = pl.ds(0, quarters - 1)
        second = remote(
            mid_in.at[r, some], mid_in.at[r, some], mid_send.at[r], mid_recv.at[r], dp, code
        )
        second.wait_recv()
        value = -join(mid_in[r])
        row_src[r] = value
        for _, to in mates:
            remote(
                row_src.at[r], row_in.at[r, share], row_send.at[r], row_recv.at[r, share], dp, to
            ).start()
        row_in[r, share] = value

    def row_arrives(r, some):
        for owner in range(some[0] // held, some[-1] // held + 1):

            @pl.when(share != owner)
            def _():
                remote(
                    row_src.at[r],
                    row_in.at[r, owner],
                    row_send.at[r],
                    row_recv.at[r, owner],
                    dp,
                    code,
                ).wait_recv()

            for i in range(held):
                for t in range(block_tiles):
                    row_b[(owner * held + i) * block_tiles + t] = jnp.broadcast_to(
                        row_in[r, owner, i, t : t + 1, :], (SUB, LANES)
                    )

    def row_sent(r):
        others, some = pl.ds(0, shares - 1), pl.ds(0, quarters - 1)
        remote(
            lse_src.at[r, others], lse_in.at[r, others], lse_send.at[r], lse_recv.at[r], dp, code
        ).wait_send()
        remote(
            mid_in.at[r, some], mid_in.at[r, some], mid_send.at[r], mid_recv.at[r], dp, code
        ).wait_send()
        remote(
            row_in.at[r, others], row_in.at[r, others], row_send.at[r], row_recv.at[r, 0], dp, code
        ).wait_send()

    def col_update(r, target):
        def one_tile(j, some):
            span = pl.ds(pl.multiple_of(j * SUB, SUB), SUB)
            tiles_of = pl.ds(some[0] * block_tiles, len(some) * block_tiles)
            x = cells[tiles_of, span, :] + row_b[tiles_of]
            x = x.reshape(len(some), block_tiles, SUB, LANES)
            at = [jnp.full((SUB, LANES), places[b], jnp.int32) for b in some]
            tops = [jnp.max(x[i], axis=0) for i in range(len(some))]
            peaks, olds = [], []
            for w in range(3):
                kept = [jnp.where(at[i] == w, tops[i], LOWEST) for i in range(len(some))]
                if some[0] > 0:
                    olds.append(peak[w, span, :])
                    kept.append(olds[w])
                peaks.append(functools.reduce(jnp.maximum, kept))
            sums = []
            for i in range(len(some)):
                top = jnp.where(at[i] == 0, peaks[0], jnp.where(at[i] == 1, peaks[1], peaks[2]))
                sums.append(jnp.sum(jnp.exp2(x[i] - top[None]), axis=0))
            for w in range(3):
                kept = [jnp.where(at[i] == w, sums[i], 0.0) for i in range(len(some))]
                if some[0] > 0:
                    kept.append(total[w, span, :] * jnp.exp2(olds[w] - peaks[w]))
                peak[w, span, :] = peaks[w]
                total[w, span, :] = functools.reduce(jnp.add, kept)

        def tile_loop(first, last, some):
            def two_tiles(j, carry):
                one_tile(2 * j, some)
                one_tile(2 * j + 1, some)
                return carry

            lax.fori_loop(first // 2, last // 2, two_tiles, 0)

        half_tiles = LANES // SUB
        early, late = range(blocks // 2), range(blocks // 2, blocks)
        row_arrives(r, early)
        tile_loop(0, size // SUB, early)
        row_arrives(r, late)
        mines, copies = [], []
        for h in range(halves):
            tile_loop(h * half_tiles, (h + 1) * half_tiles, late)
            span = slice(h * LANES, (h + 1) * LANES)
            tops, sums = peak[:, span, :], total[:, span, :]
            m = jnp.max(tops, axis=2, keepdims=True)
            s = jnp.sum(sums * jnp.exp2(tops - m), axis=2, keepdims=True)
            mine = to_lanes(jnp.broadcast_to(m, tops.shape)) + jnp.log2(
                to_lanes(jnp.broadcast_to(s, sums.shape))
            )
            mines.append(mine)
            for w in range(3):
                col_src[r, h, w] = mine[w : w + 1]
            for slot, (step, start, count, there) in enumerate(
                ((-2, 0, 1, col_r2), (2, 2, 1, col_l2), (-1, 0, 2, col_r1), (1, 1, 2, col_l1))
            ):
                copies.append(
                    remote(
                        col_src.at[r, h, pl.ds(start, count)],
                        there.at[r, h],
                        col_send.at[r, h, slot],
                        col_recv.at[r, h, slot],
                        dp_near[step],
                        code,
                    )
                )
                copies[-1].start()
        for h in range(halves):
            for copy in copies[4 * h : 4 * h + 4]:
                copy.wait_recv()
            mine, l1, r1 = mines[h], col_l1[r, h], col_r1[r, h]
            sets = (
                (col_l2[r, h, 0], l1[0], mine[0:1]),
                (l1[1], mine[1:2], r1[0]),
                (mine[2:3], r1[1], col_r2[r, h, 0]),
            )
            for w, terms in enumerate(sets):
                m = functools.reduce(jnp.maximum, terms)
                s = functools.reduce(jnp.add, [jnp.exp2(term - m) for term in terms])
                value = target - (m + jnp.log2(s))
                col_b[w, h * LANES : (h + 1) * LANES, :] = to_column(value)
        for copy in copies:
            copy.wait_send()
        row_sent(r)

    target = math.log2((rows * n_dp) / (size * n_dp * n_code))

    def sweep(r, carry):
        row_update(r)
        col_update(r, target)
        return carry

    lax.fori_loop(0, ROUNDS, sweep, 0)
    row_update(ROUNDS)
    pack = 2 * SUB

    def weigh(some):
        def body(j, carry):
            span = pl.ds(pl.multiple_of(j * pack, pack), pack)
            sums = [jnp.zeros((2, SUB, LANES), jnp.float32) for w in range(3)]
            for b in some:
                g = col_b[places[b], span, :].reshape(2, SUB, LANES)
                here = jnp.zeros((2, SUB, LANES), jnp.float32)
                for t in range(block_tiles):
                    d = b * block_tiles + t
                    x = cells[d, span, :].reshape(2, SUB, LANES) + row_b[d][None] + g
                    value = jnp.exp2(x)
                    here = here + value
                    low = value.reshape(pack, LANES).astype(jnp.bfloat16)
                    weight[b, span, t * LANES : (t + 1) * LANES] = low
                at = jnp.full((2, SUB, LANES), places[b], jnp.int32)
                for w in range(3):
                    sums[w] = sums[w] + jnp.where(at == w, here, 0.0)
            for w in range(3):
                part = sums[w].reshape(pack, LANES)
                total[w, span, :] = part if some[0] == 0 else total[w, span, :] + part
            return carry

        lax.fori_loop(0, size // pack, body, 0)

    for some in (range(blocks // 2), range(blocks // 2, blocks)):
        row_arrives(ROUNDS, some)
        weigh(some)
    row_sent(ROUNDS)

    mass = jnp.sum(total[...], axis=2, keepdims=True)
    mass = jnp.broadcast_to(mass, total.shape)
    for h in range(halves):
        part = to_lanes(mass[:, h * LANES : (h + 1) * LANES, :])
        mass_src[:, h, :] = part.astype(jnp.bfloat16).astype(jnp.float32)
    mass_copies = [
        remote(
            mass_src.at[pl.ds(2 * s, 1)],
            mass_in.at[1 - s],
            mass_send.at[s],
            mass_recv.at[1 - s],
            dp_near[2 * s - 1],
            code,
        )
        for s in range(2)
    ]
    for copy in mass_copies:
        copy.start()

    def columns(n):
        return pl.ds(pl.multiple_of(n * piece, piece), piece)

    def num_copy(s, n):
        land = 1 - ups[s]
        return remote(
            num_src.at[s, n],
            num_in.at[land, n],
            num_send.at[s, n],
            num_recv.at[land, n],
            sides[s],
            code,
        )

    def numerators(n, carry):
        products = []
        for b in range(blocks):
            product = jnp.dot(
                weight[b],
                feat[b * block_rows : (b + 1) * block_rows, columns(n)],
                preferred_element_type=jnp.float32,
            )
            products.append((jnp.full(product.shape, places[b], jnp.int32), product))

        def window_sum(w):
            kept = [jnp.where(at == w, product, 0.0) for at, product in products]
            return functools.reduce(jnp.add, kept).astype(jnp.bfloat16)

        for s in range(2):
            num_src[s, n] = window_sum(2 * ups[s])
            num_copy(s, n).start()
        num_own[n] = window_sum(1)
        return carry

    lax.fori_loop(0, PIECES, numerators, 0)

    for s in range(2):
        remote(
            mass_src.at[pl.ds(0, 1)], mass_in.at[s], mass_send.at[s], mass_recv.at[s], dp, code
        ).wait_recv()
    for copy in mass_copies:
        copy.wait_send()
    mass_ref[...] = mass_in[0, 0] + mass_src[1] + mass_in[1, 0]

    def finish(n, carry):
        for s in range(2):
            remote(
                num_src.at[s, n], num_in.at[s, n], num_send.at[s, n], num_recv.at[s, n], dp, code
            ).wait()
        own = num_own[n].astype(jnp.float32)
        whole_ref[n] = (
            num_in[0, n].astype(jnp.float32) + own + num_in[1, n].astype(jnp.float32)
        )
        return carry

    lax.fori_loop(0, PIECES, finish, 0)


def divide(whole_ref, mass_in_ref, out_ref, mass_ref):
    size, piece = whole_ref.shape[1], whole_ref.shape[2]
    eye = lax.broadcasted_iota(jnp.int32, (LANES, LANES), 0) == lax.broadcasted_iota(
        jnp.int32, (LANES, LANES), 1
    )
    mass_ref[...] = mass_in_ref[...]
    for h in range(size // LANES):
        row = jnp.broadcast_to(mass_in_ref[h : h + 1, :], (LANES, LANES))
        column = jnp.sum(jnp.where(eye, row, 0.0), axis=1, keepdims=True)
        span = slice(h * LANES, (h + 1) * LANES)
        for n in range(PIECES):
            value = whole_ref[n, span, :] / column
            out_ref[span, n * piece : (n + 1) * piece] = value.astype(out_ref.dtype)


def solution(mesh):
    n_dp, n_code = mesh.shape["dp"], mesh.shape["code"]

    def local(features, centroids, block_lists):
        rows, width = features.shape
        size = centroids.shape[0]
        tiles = rows // LANES
        blocks = block_lists.shape[0]
        block_tiles = tiles // blocks
        shares = NEAR * (n_code // Z)
        mine = (blocks // shares, block_tiles, LANES)
        halves = size // LANES
        piece = width // PIECES
        updates = ROUNDS + 1
        f32, bf16 = jnp.float32, jnp.bfloat16
        dma = pltpu.SemaphoreType.DMA
        whole, mass = pl.pallas_call(
            functools.partial(kernel, n_dp, n_code),
            out_shape=(
                jax.ShapeDtypeStruct((PIECES, size, piece), f32),
                jax.ShapeDtypeStruct((halves, LANES), f32),
            ),
            in_specs=[
                pl.BlockSpec(memory_space=pltpu.SMEM),
                pl.BlockSpec(memory_space=pl.ANY),
                pl.BlockSpec(memory_space=pl.ANY),
            ],
            out_specs=(
                pl.BlockSpec(memory_space=pltpu.VMEM),
                pl.BlockSpec(memory_space=pltpu.VMEM),
            ),
            scratch_shapes=[
                pltpu.VMEM((rows, width), bf16),
                pltpu.VMEM((3, size, width), bf16),
                pltpu.VMEM((tiles, size, LANES), f32),
                pltpu.VMEM((tiles, SUB, LANES), f32),
                pltpu.VMEM((3, size, LANES), f32),
                pltpu.VMEM((3, size, LANES), f32),
                pltpu.VMEM((3, size, LANES), f32),
                pltpu.VMEM((blocks, size, rows // blocks), bf16),
                pltpu.SMEM((blocks,), jnp.int32),
                pltpu.VMEM((updates, shares, *mine), f32),
                pltpu.VMEM((updates, shares, *mine), f32),
                pltpu.VMEM((updates, *mine), f32),
                pltpu.VMEM((updates, Z // NEAR, *mine), f32),
                pltpu.VMEM((updates, *mine), f32),
                pltpu.VMEM((updates, shares, *mine), f32),
                pltpu.VMEM((ROUNDS, halves, 3, 1, LANES), f32),
                pltpu.VMEM((ROUNDS, halves, 1, 1, LANES), f32),
                pltpu.VMEM((ROUNDS, halves, 2, 1, LANES), f32),
                pltpu.VMEM((ROUNDS, halves, 2, 1, LANES), f32),
                pltpu.VMEM((ROUNDS, halves, 1, 1, LANES), f32),
                pltpu.VMEM((3, halves, LANES), f32),
                pltpu.VMEM((2, 1, halves, LANES), f32),
                pltpu.VMEM((2, PIECES, size, piece), bf16),
                pltpu.VMEM((2, PIECES, size, piece), bf16),
                pltpu.VMEM((PIECES, size, piece), bf16),
                dma((blocks,)),
                dma,
                dma((2,)),
                dma((2,)),
                dma((updates,)),
                dma((updates,)),
                dma((updates,)),
                dma((updates,)),
                dma((updates,)),
                dma((updates, shares)),
                dma((ROUNDS, halves, 4)),
                dma((ROUNDS, halves, 4)),
                dma((2,)),
                dma((2,)),
                dma((2, PIECES)),
                dma((2, PIECES)),
            ],
            compiler_params=pltpu.CompilerParams(
                collective_id=0, has_side_effects=True, vmem_limit_bytes=56 * 1024 * 1024
            ),
            cost_estimate=pl.CostEstimate(
                flops=8 * rows * size * width,
                bytes_accessed=2 * (rows + 2 * size) * width,
                transcendentals=8 * rows * size,
            ),
            name="balanced_kmeans",
        )(block_lists, features, centroids)
        new_centroids, mass = pl.pallas_call(
            divide,
            out_shape=(
                jax.ShapeDtypeStruct((size, width), bf16),
                jax.ShapeDtypeStruct((halves, LANES), f32),
            ),
            cost_estimate=pl.CostEstimate(
                flops=size * width, bytes_accessed=6 * size * width, transcendentals=0
            ),
            name="divide",
        )(whole, mass)
        return new_centroids, mass.reshape(size)

    return jax.shard_map(
        local,
        mesh=mesh,
        in_specs=(P("dp", None), P(("code", "dp"), None), P("dp", None)),
        out_specs=(P(("code", "dp"), None), P(("code", "dp"))),
        check_vma=False,
    )
```
